32 devices in a mesh: dp: 8 (over y, x, core), inner: 4 (over z).
Axes of the slice: x: 2, y: 2, z: 4, core: 2. Of those that a mesh axis runs over, the one named last changes fastest.
Arguments:
- queries: bfloat16 [32, 512, 1024], P('dp', 'inner'), may hold values from -6 to 6
- passages: bfloat16 [32, 512, 1024], P('dp', 'inner'), may hold values from -6 to 6
- neg_lists: int32 [32, 8], replicated, may hold values from 0 to 31, as said below
Outputs:
- mean_loss: float32 [], replicated
- query_grad: bfloat16 [32, 512, 1024], P('dp', 'inner')
- passage_grad: bfloat16 [32, 512, 1024], P('dp', 'inner')
The draws below stay inside these ranges and needn't reach their ends.
Inputs may be any that keep to these rules, and one draw needn't show every extreme that they name: `neg_lists`: each row lists 8 different passage blocks, none from the row's own group (blocks with the same id // 4). The blocks that the rows of one group list include at least one and at most 2 blocks of every other group; in every draw some group lists exactly 2 blocks of every other group.
All inputs are finite; a program needn't handle non-finite values.
Results may differ from the reference program's by a relative error of at most 0.009.
Values may be sent and summed in bfloat16 or wider, within the bound.
No kernel may reach another device: no remote copies, remote signals or barrier semaphores. Data moves between devices by JAX's collectives and lax.ppermute only.
A program may use at most 128 MiB of HBM per device.

```python
import math
import jax
import jax.numpy as jnp
from jax import lax

D = 1024
ROWS = 512
K = 8
CAP = 2
GB = 4
NBLK = 32
N_INNER = 4


def embed_pair(key):
    keys_list = [jax.random.fold_in(key, number) for number in (101, 102, 103, 104, 105)]
    shape_full = (NBLK, ROWS, D)
    base_rows = jnp.clip(jax.random.normal(keys_list[0], shape_full, jnp.float32), -4.0, 4.0)
    noise_rows = jnp.clip(jax.random.normal(keys_list[1], shape_full, jnp.float32), -4.0, 4.0)
    tilt_factor = 0.3
    block_pos = (jnp.arange(NBLK, dtype=jnp.float32) + 1.0) / NBLK
    row_index = jnp.arange(ROWS, dtype=jnp.int32)
    row_pos = (row_index.astype(jnp.float32) + 1.0) / ROWS
    mixing = tilt_factor * block_pos[:, None, None] * row_pos[None, :, None]
    query_rows = jnp.clip(mixing * base_rows + noise_rows, -6.0, 6.0)
    passage_rows = base_rows
    return (query_rows, passage_rows)


def draw_queries(key, part):
    return embed_pair(key)[0].astype(jnp.bfloat16)


def draw_passages(key, part):
    return embed_pair(key)[1].astype(jnp.bfloat16)


def pick_row(ordered_row, index_row):
    return ordered_row[index_row]


def draw_neg_lists(key, part):
    groups = NBLK // GB
    keys_list = [jax.random.fold_in(key, number) for number in (201, 202, 203, 204, 205)]
    group_ids = jnp.arange(groups, dtype=jnp.int32)
    slot_counts = jax.random.randint(keys_list[0], (groups, groups), 1, CAP + 1)
    full_group = jax.random.randint(keys_list[1], (), 0, groups)
    offset_pick = jax.random.randint(keys_list[2], (), 1, groups)
    slot_counts = jnp.where(group_ids[:, None] == full_group, CAP, slot_counts)
    slot_counts = jnp.where(group_ids[None, :] == (group_ids[:, None] + offset_pick) % groups, CAP, slot_counts)
    slot_counts = jnp.where(group_ids[None, :] == group_ids[:, None], 0, slot_counts)
    raw_bits = jax.random.randint(keys_list[3], (groups, groups, GB), 0, 1 << 20)
    local_order = jnp.argsort(raw_bits * GB + jnp.arange(GB, dtype=jnp.int32), axis=-1).astype(jnp.int32)
    cand_blocks = group_ids[None, :, None] * GB + local_order[:, :, :CAP]
    live_slots = jnp.arange(CAP, dtype=jnp.int32)[None, None, :] < slot_counts[:, :, None]
    cand_blocks = cand_blocks.reshape(groups, groups * CAP)
    live_slots = live_slots.reshape(groups, groups * CAP)
    raw_order = jax.random.randint(keys_list[4], (groups, groups * CAP), 0, 1 << 20)
    sort_keys = raw_order * (groups * CAP) + jnp.arange(groups * CAP, dtype=jnp.int32)
    sort_keys = jnp.where(live_slots, sort_keys, sort_keys + (1 << 20) * (groups * CAP))
    sort_order = jnp.argsort(sort_keys, axis=-1)
    ordered = jnp.take_along_axis(cand_blocks, sort_order, axis=-1)
    used_count = jnp.sum(live_slots.astype(jnp.int32), axis=-1)
    positions = jnp.arange(GB, dtype=jnp.int32)[:, None] * K + jnp.arange(K, dtype=jnp.int32)[None, :]
    index_rows = (positions[None, :, :] % used_count[:, None, None]).reshape(groups, GB * K)
    picked = jax.vmap(pick_row)(ordered, index_rows)
    return picked.reshape(NBLK, K).astype(jnp.int32)


def setup_inputs(seed: int = 0) -> dict:
    splits = jax.random.split(jax.random.key(seed), 4)
    queries = draw_queries(jax.random.fold_in(splits[3], 71), 0)
    passages = draw_passages(jax.random.fold_in(splits[3], 71), 0)
    neg_lists = draw_neg_lists(jax.random.fold_in(splits[3], 71), 0)
    return {"queries": queries, "passages": passages, "neg_lists": neg_lists}


def reference(queries, passages, neg_lists):
    block_count, block_rows, embed_width = queries.shape
    pick_count = neg_lists.shape[1]
    score_scale = 1.0 / math.sqrt(embed_width)
    slice_rows = block_rows // N_INNER
    block_ids = jnp.arange(block_count, dtype=jnp.int32)
    cand_ids = jnp.concatenate([block_ids[:, None], neg_lists.astype(jnp.int32)], axis=1)

    def logits_of(block_index):
        chosen = passages[cand_ids[block_index]].reshape((pick_count + 1) * block_rows, embed_width)
        return jnp.dot(chosen, queries[block_index].T, preferred_element_type=jnp.float32) * score_scale

    def first_pass(accum, block_index):
        logits = logits_of(block_index)
        row_lse = jax.nn.logsumexp(logits, axis=0)
        col_lse = jax.nn.logsumexp(logits, axis=1).reshape(pick_count + 1, block_rows)
        chosen_ids = cand_ids[block_index]
        accum = accum.at[chosen_ids].set(jnp.logaddexp(accum[chosen_ids], col_lse))
        return (accum, row_lse)
    start_lse = jnp.full((block_count, block_rows), -jnp.inf, dtype=jnp.float32)
    passage_lse, query_lse = lax.scan(first_pass, start_lse, block_ids)
    cand_total = (pick_count + 1) * block_rows
    own_target = (jnp.arange(cand_total)[:, None] == jnp.arange(block_rows)[None, :]).astype(jnp.float32)

    def block_step(far_sum, block_index):
        logits = logits_of(block_index)
        col_lse = passage_lse[cand_ids[block_index]].reshape(cand_total)
        probs = 0.5 * jnp.exp(logits - query_lse[block_index][None, :]) + 0.5 * jnp.exp(logits - col_lse[:, None]) - own_target
        weights = probs.astype(jnp.bfloat16)
        chosen = passages[cand_ids[block_index]]
        split_weights = weights.reshape(pick_count + 1, N_INNER, slice_rows, block_rows).astype(jnp.float32)
        split_cands = chosen.reshape(pick_count + 1, N_INNER, slice_rows, embed_width).astype(jnp.float32)
        slice_parts = jnp.einsum('kicr,kicd->ird', split_weights, split_cands)
        rounded_parts = lax.optimization_barrier(slice_parts.astype(jnp.bfloat16)).astype(jnp.float32)
        query_grad = lax.optimization_barrier(jnp.sum(rounded_parts, axis=0)).astype(jnp.bfloat16)
        passage_part = jnp.einsum('cr,rd->cd', weights.astype(jnp.float32), queries[block_index].astype(jnp.float32))
        passage_part = passage_part.reshape(pick_count + 1, block_rows, embed_width)
        far_sum = far_sum.at[neg_lists[block_index].astype(jnp.int32)].add(passage_part[1:])
        return (far_sum, (query_grad, passage_part[0]))

    def group_step(group_total, group_index):
        members = group_index * GB + jnp.arange(GB, dtype=jnp.int32)
        start_far = jnp.zeros((block_count, block_rows, embed_width), jnp.float32)
        far_sum, outputs = lax.scan(block_step, start_far, members)
        group_total = group_total + lax.optimization_barrier(far_sum.astype(jnp.bfloat16)).astype(jnp.float32)
        return (group_total, outputs)
    group_ids = jnp.arange(block_count // GB, dtype=jnp.int32)
    start_total = jnp.zeros((block_count, block_rows, embed_width), jnp.float32)
    group_total, (query_all, own_all) = lax.scan(group_step, start_total, group_ids)
    query_grad = query_all.reshape(block_count, block_rows, embed_width)
    passage_grad = (group_total + own_all.reshape(block_count, block_rows, embed_width)).astype(jnp.bfloat16)
    own_scores = jnp.einsum('brd,brd->br', queries.astype(jnp.float32), passages.astype(jnp.float32)) * score_scale
    mean_loss = (jnp.sum(query_lse - own_scores) + jnp.sum(passage_lse - own_scores)) / (2.0 * block_count * block_rows)
    return (mean_loss, query_grad, passage_grad)
```

```python
import functools
import math

import jax
import jax.numpy as jnp
from jax import lax
from jax.experimental import pallas as pl
from jax.experimental.pallas import tpu as pltpu
from jax.sharding import PartitionSpec as P

CAP = 2
NEG_FILL = -1e30
LOG2E = math.log2(math.e)
LN2 = math.log(2.0)
ANY = pl.BlockSpec(memory_space=pl.ANY)
SMEM = pl.BlockSpec(memory_space=pltpu.SMEM)
VMEM = pl.BlockSpec(memory_space=pltpu.VMEM)
VMEM_LIMIT = 48 * 1024 * 1024


def slot_tables(neg_lists, groups, per_group, slot_depth):
    block_count = neg_lists.shape[0]
    block_ids = jnp.arange(block_count, dtype=jnp.int32)
    named = jnp.any(neg_lists[:, :, None] == block_ids[None, None, :], axis=1)
    present = jnp.any(named.reshape(groups, per_group, block_count), axis=1)
    present = present.reshape(groups, groups, per_group).astype(jnp.int32)
    slot_ranks = jnp.cumsum(present, axis=2) - 1
    slot_ids = jnp.arange(slot_depth, dtype=jnp.int32)
    hits = (present[..., None] == 1) & (slot_ranks[..., None] == slot_ids[None, None, None, :])
    local_ids = jnp.arange(per_group, dtype=jnp.int32)
    slot_block = jnp.sum(jnp.where(hits, local_ids[None, None, :, None], 0), axis=2)
    slot_live = jnp.any(hits, axis=2)
    return (slot_ranks, slot_block, slot_live)


def join_log2(a, b):
    return jnp.maximum(a, b) + jnp.log2(1.0 + jnp.exp2(-jnp.abs(a - b)))


def row_tile(rows):
    return math.gcd(rows, 256)


class Fetch:
    def __init__(self, first, inner, picks, pos_ref, slot_ref, own_q, from_left, from_right, own_p, far_p,
                 cands, whole_q, sems):
        self.first, self.inner, self.picks = first, inner, picks
        self.pos_ref, self.slot_ref = pos_ref, slot_ref
        self.own_q, self.from_left, self.from_right = own_q, from_left, from_right
        self.own_p, self.far_p = own_p, far_p
        self.cands, self.whole_q, self.sems = cands, whole_q, sems
        self.rows = own_q.shape[1]

    def cand_copy(self, b, buf, k):
        block = self.first + b
        if k == 0:
            src = self.own_p.at[block]
        else:
            src = self.far_p.at[self.slot_ref[block * self.picks + k - 1]]
        dst = self.cands.at[buf, pl.ds(k * self.rows, self.rows)]
        return pltpu.make_async_copy(src, dst, self.sems.at[buf, k])

    def query_copy(self, src, buf, pos, k):
        dst = self.whole_q.at[buf, pl.ds(pl.multiple_of(pos * self.rows, self.rows), self.rows)]
        return pltpu.make_async_copy(src, dst, self.sems.at[buf, self.picks + 1 + k])

    def start_q(self, b, buf):
        pos = self.pos_ref[0]
        self.query_copy(self.own_q.at[self.first + b], buf, pos, 0).start()
        for k in range(1, self.inner):
            @pl.when(pos >= k)
            def _():
                self.query_copy(self.from_left[k - 1].at[b], buf, pos - k, k).start()

            @pl.when(pos < k)
            def _():
                self.query_copy(
                    self.from_right[self.inner - k - 1].at[b], buf, pos - k + self.inner, k
                ).start()

    def start(self, b, buf):
        self.start_q(b, buf)
        for k in range(self.picks + 1):
            self.cand_copy(b, buf, k).start()

    def wait_q(self, b, buf):
        for k in range(self.inner):
            self.query_copy(self.own_q.at[self.first + b], buf, k, k).wait()

    def wait(self, b, buf):
        self.wait_q(b, buf)
        for k in range(self.picks + 1):
            self.cand_copy(b, buf, 0 if k == 0 else k).wait()


def dot_t(a, b):
    return lax.dot_general(a, b, (((1,), (1,)), ((), ())), preferred_element_type=jnp.float32)


def forward_kernel(first, count, inner, picks, scale, *refs):
    pos_ref, slot_ref, id_ref, own_q = refs[:4]
    from_left = refs[4:3 + inner]
    from_right = refs[3 + inner:2 + 2 * inner]
    own_p, far_p, col_in, row_out, col_out, cands, whole_q, sems = refs[2 + 2 * inner:]
    rows = own_q.shape[1]
    full = rows * inner
    tile = row_tile(full)
    fetch = Fetch(first, inner, picks, pos_ref, slot_ref, own_q, from_left, from_right, own_p, far_p,
                  cands, whole_q, sems)
    fetch.start(0, 0)
    col_out[...] = col_in[...]
    for b in range(count):
        buf = b % 2
        if b + 1 < count:
            fetch.start(b + 1, 1 - buf)
        fetch.wait(b, buf)
        block_col = None
        for t in range(full // tile):
            logits = dot_t(whole_q[buf, t * tile:(t + 1) * tile, :], cands[buf]) * scale
            peak = jnp.max(logits, axis=1, keepdims=True)
            mass = jnp.sum(jnp.exp2(logits - peak), axis=1, keepdims=True)
            row_lse = jnp.broadcast_to(peak + jnp.log2(mass), (tile, 128))
            row_out[b:b + 1, t * tile:(t + 1) * tile] = row_lse.T[0:1, :]
            col_peak = jnp.max(logits, axis=0, keepdims=True)
            col_mass = jnp.sum(jnp.exp2(logits - col_peak), axis=0, keepdims=True)
            col_lse = col_peak + jnp.log2(col_mass)
            block_col = col_lse if block_col is None else join_log2(block_col, col_lse)
        for k in range(picks + 1):
            row = pl.ds(id_ref[(first + b) * (picks + 1) + k], 1)
            col_out[row, :] = join_log2(col_out[row, :], block_col[:, k * rows:(k + 1) * rows])


def query_kernel(first, count, inner, picks, scale, *refs):
    pos_ref, slot_ref, id_ref, own_q = refs[:4]
    from_left = refs[4:3 + inner]
    from_right = refs[3 + inner:2 + 2 * inner]
    own_p, far_p, row_lse, col_lse, dq_out, w_out, cands, whole_q, sems = refs[2 + 2 * inner:]
    rows = own_q.shape[1]
    full = rows * inner
    tile = row_tile(full)
    fetch = Fetch(first, inner, picks, pos_ref, slot_ref, own_q, from_left, from_right, own_p, far_p,
                  cands, whole_q, sems)
    fetch.start(0, 0)
    pos = pos_ref[0]
    for b in range(count):
        buf = b % 2
        if b + 1 < count:
            fetch.start(b + 1, 1 - buf)
        col = jnp.concatenate(
            [
                col_lse[pl.ds(id_ref[(first + b) * (picks + 1) + k], 1), :]
                for k in range(picks + 1)
            ],
            axis=1,
        ) + 1.0
        row = jnp.broadcast_to(row_lse[first + b:first + b + 1, :] + 1.0, (128, full)).T
        fetch.wait(b, buf)
        for t in range(full // tile):
            part = slice(t * tile, (t + 1) * tile)
            logits = dot_t(whole_q[buf, part, :], cands[buf]) * scale
            probs = jnp.exp2(logits - row[part, 0:1]) + jnp.exp2(logits - col)
            r_id = lax.broadcasted_iota(jnp.int32, (tile, rows), 0) + t * tile - pos * rows
            c_id = lax.broadcasted_iota(jnp.int32, (tile, rows), 1)
            target = jnp.where(r_id == c_id, 1.0, 0.0)
            w_out[b, part, 0:rows] = (probs[:, 0:rows] - target).astype(jnp.bfloat16)
            w_out[b, part, rows:] = probs[:, rows:].astype(jnp.bfloat16)
            grad = jnp.dot(w_out[b, part, :], cands[buf], preferred_element_type=jnp.float32)
            dq_out[b, part, :] = grad.astype(jnp.bfloat16)


def passage_kernel(chunk, chunks, inner, picks, *refs):
    pos_ref, slot_ref, own_q = refs[:3]
    place = 3
    lefts, rights = [], []
    for _ in range(chunks):
        lefts.append(refs[place:place + inner - 1])
        rights.append(refs[place + inner - 1:place + 2 * inner - 2])
        place += 2 * inner - 2
    w_refs = refs[place:place + chunks]
    own_out, far_out, far_acc, w_buf, whole_q, sems = refs[place + chunks:]
    rows = own_q.shape[1]
    total = chunk * chunks

    def fetcher(b):
        c = b // chunk
        return Fetch(c * chunk, inner, picks, pos_ref, slot_ref, own_q, lefts[c], rights[c], None, None,
                     None, whole_q, sems), b % chunk

    def w_copy(b, buf):
        return pltpu.make_async_copy(w_refs[b // chunk].at[b % chunk], w_buf.at[buf], sems.at[buf, 0])

    def start(b):
        f, local = fetcher(b)
        f.start_q(local, b % 2)
        w_copy(b, b % 2).start()

    start(0)
    far_acc[...] = jnp.zeros_like(far_acc)
    for b in range(total):
        buf = b % 2
        if b + 1 < total:
            start(b + 1)
        f, local = fetcher(b)
        f.wait_q(local, buf)
        w_copy(b, buf).wait()
        for k in range(picks + 1):
            part = lax.dot_general(
                w_buf[buf, :, k * rows:(k + 1) * rows], whole_q[buf],
                (((0,), (0,)), ((), ())), preferred_element_type=jnp.float32,
            )
            if k == 0:
                own_out[b] = part
            else:
                slot = slot_ref[b * picks + k - 1]
                far_acc[slot] = far_acc[slot] + part
    far_out[...] = far_acc[...].astype(jnp.bfloat16)


def finish_kernel(slots, dest_ref, own_ref, far_ref, out_ref, acc):
    acc[0:own_ref.shape[0]] = own_ref[...]
    for e in range(slots):
        dest = dest_ref[e]
        acc[dest] = acc[dest] + far_ref[e].astype(jnp.float32)
    out_ref[...] = acc[0:own_ref.shape[0]].astype(jnp.bfloat16)


def butterfly(value, axis, size, join):
    step = 1
    while step < size:
        other = lax.ppermute(value, axis, [(i, i ^ step) for i in range(size)])
        value = join(value, other)
        step *= 2
    return value


def body(queries, passages, neg_lists):
    per_group, rows, width = queries.shape
    picks = neg_lists.shape[1]
    blocks = neg_lists.shape[0]
    groups = lax.axis_size("dp")
    inner = lax.axis_size("inner")
    full = rows * inner
    cand_rows = (picks + 1) * rows
    slot_count = groups * CAP
    scale = 1.0 / math.sqrt(width)
    my_group = lax.axis_index("dp")
    pos = lax.axis_index("inner")
    chunks = 2
    chunk = per_group // chunks

    slot_ranks, slot_block, slot_live = slot_tables(neg_lists, groups, per_group, CAP)
    listed = lax.dynamic_slice_in_dim(neg_lists, my_group * per_group, per_group, 0)
    my_ranks = lax.dynamic_index_in_dim(slot_ranks, my_group, 0, keepdims=False)
    slot_of = (listed // per_group) * CAP + my_ranks[listed // per_group, listed % per_group]
    slot_flat = slot_of.reshape(-1)
    own_ids = my_group * per_group + jnp.arange(per_group, dtype=jnp.int32)
    id_flat = jnp.concatenate([own_ids[:, None], listed], axis=1).reshape(-1)
    pos_arr = pos.reshape(1)
    sends_for = lax.dynamic_index_in_dim(slot_block, my_group, 1, keepdims=False)
    live_for = lax.dynamic_index_in_dim(slot_live, my_group, 1, keepdims=False)

    lefts = [[] for _ in range(chunks)]
    rights = [[] for _ in range(chunks)]
    moving_r = [queries[c * chunk:(c + 1) * chunk] for c in range(chunks)]
    moving_l = list(moving_r)
    for s in range(1, inner):
        for c in range(chunks):
            moving_r[c] = lax.ppermute(moving_r[c], "inner", [(i, i + 1) for i in range(s - 1, inner - 1)])
            moving_l[c] = lax.ppermute(moving_l[c], "inner", [(i, i - 1) for i in range(inner - s, 0, -1)])
            lefts[c].append(moving_r[c])
            rights[c].append(moving_l[c])

    outgoing = passages[sends_for]
    arrived = lax.all_to_all(outgoing, "dp", split_axis=0, concat_axis=0, tiled=True)
    arrived = arrived.reshape(slot_count, rows, width)

    fetch_scratch = [
        pltpu.VMEM((2, cand_rows, width), jnp.bfloat16),
        pltpu.VMEM((2, full, width), jnp.bfloat16),
        pltpu.SemaphoreType.DMA((2, picks + 1 + inner)),
    ]
    params = pltpu.CompilerParams(vmem_limit_bytes=VMEM_LIMIT)
    tile_flops = 2 * full * cand_rows * width

    col = jnp.full((blocks, rows), NEG_FILL, jnp.float32)
    row_parts = []
    for c in range(chunks):
        row_part, col = pl.pallas_call(
            functools.partial(forward_kernel, c * chunk, chunk, inner, picks, scale * LOG2E),
            out_shape=(
                jax.ShapeDtypeStruct((chunk, full), jnp.float32),
                jax.ShapeDtypeStruct((blocks, rows), jnp.float32),
            ),
            in_specs=[SMEM] * 3 + [ANY] * (2 * inner + 1) + [VMEM],
            out_specs=(VMEM, VMEM),
            scratch_shapes=fetch_scratch,
            compiler_params=params,
            cost_estimate=pl.CostEstimate(
                flops=chunk * tile_flops, bytes_accessed=chunk * (full + cand_rows) * width * 2, transcendentals=0
            ),
            name=f"forward_{c}",
        )(pos_arr, slot_flat, id_flat, queries, *lefts[c], *rights[c], passages, arrived, col)
        row_parts.append(row_part)
    row = jnp.concatenate(row_parts, axis=0)
    col_lse = butterfly(col, "dp", groups, join_log2)
    row_lse = butterfly(row, "inner", inner, join_log2)

    dq, weights = [], []
    for c in range(chunks):
        grad, weight = pl.pallas_call(
            functools.partial(query_kernel, c * chunk, chunk, inner, picks, scale * LOG2E),
            out_shape=(
                jax.ShapeDtypeStruct((chunk, full, width), jnp.bfloat16),
                jax.ShapeDtypeStruct((chunk, full, cand_rows), jnp.bfloat16),
            ),
            in_specs=[SMEM] * 3 + [ANY] * (2 * inner + 1) + [VMEM, VMEM],
            out_specs=(VMEM, VMEM),
            scratch_shapes=fetch_scratch,
            compiler_params=params,
            cost_estimate=pl.CostEstimate(
                flops=2 * chunk * tile_flops, bytes_accessed=chunk * (full + cand_rows) * width * 4, transcendentals=0
            ),
            name=f"query_{c}",
        )(pos_arr, slot_flat, id_flat, queries, *lefts[c], *rights[c], passages, arrived, row_lse, col_lse)
        dq.append(grad)
        weights.append(weight)

    rings = []
    for c in range(chunks):
        rings += [*lefts[c], *rights[c]]
    own_grad, far_grad = pl.pallas_call(
        functools.partial(passage_kernel, chunk, chunks, inner, picks),
        out_shape=(
            jax.ShapeDtypeStruct((per_group, rows, width), jnp.float32),
            jax.ShapeDtypeStruct((slot_count, rows, width), jnp.bfloat16),
        ),
        in_specs=[SMEM] * 2 + [ANY] * (1 + chunks * (2 * inner - 1)),
        out_specs=(VMEM, VMEM),
        scratch_shapes=[
            pltpu.VMEM((slot_count, rows, width), jnp.float32),
            pltpu.VMEM((2, full, cand_rows), jnp.bfloat16),
            pltpu.VMEM((2, full, width), jnp.bfloat16),
            pltpu.SemaphoreType.DMA((2, picks + 1 + inner)),
        ],
        compiler_params=params,
        cost_estimate=pl.CostEstimate(
            flops=per_group * tile_flops, bytes_accessed=per_group * (full + cand_rows) * width * 4, transcendentals=0
        ),
        name="passage",
    )(pos_arr, slot_flat, queries, *rings, *weights)

    f32 = jnp.float32
    query_parts = []
    for c in range(chunks):
        parts = dq[c].reshape(chunk, inner, rows, width)

        def part_of(target):
            target = jnp.clip(target, 0, inner - 1)
            return lax.dynamic_index_in_dim(parts, target, 1, keepdims=False).astype(f32)

        going_r = going_l = None
        for s in range(1, inner):
            out_r = part_of(inner - s + pos)
            out_l = part_of(pos + s - inner)
            if going_r is not None:
                out_r = out_r + going_r
                out_l = out_l + going_l
            going_r = lax.ppermute(out_r.astype(jnp.bfloat16), "inner", [(i, i + 1) for i in range(s)])
            going_l = lax.ppermute(
                out_l.astype(jnp.bfloat16), "inner", [(i, i - 1) for i in range(inner - 1, inner - 1 - s, -1)]
            )
        query_parts.append((part_of(pos) + going_r + going_l).astype(jnp.bfloat16))
    query_grad = jnp.concatenate(query_parts, axis=0)

    returned = lax.all_to_all(
        far_grad.reshape(groups, CAP, rows, width), "dp", split_axis=0, concat_axis=0, tiled=True
    ).reshape(slot_count, rows, width)
    dest = jnp.where(live_for, sends_for, per_group).reshape(-1)
    passage_grad = pl.pallas_call(
        functools.partial(finish_kernel, slot_count),
        out_shape=jax.ShapeDtypeStruct((per_group, rows, width), jnp.bfloat16),
        in_specs=[SMEM, VMEM, VMEM],
        out_specs=VMEM,
        scratch_shapes=[pltpu.VMEM((per_group + 1, rows, width), f32)],
        compiler_params=params,
        name="finish",
    )(dest, own_grad, returned)

    own_scores = jnp.einsum("lrd,lrd->lr", queries, passages, preferred_element_type=f32) * scale
    my_row = lax.dynamic_slice_in_dim(row_lse, pos * rows, rows, 1) * LN2
    my_col = lax.dynamic_slice_in_dim(col_lse, my_group * per_group, per_group, 0) * LN2
    loss = jnp.sum(my_row - own_scores) + jnp.sum(my_col - own_scores)
    loss = butterfly(loss.reshape(1, 1), "dp", groups, jnp.add)
    loss = butterfly(loss, "inner", inner, jnp.add)
    mean_loss = loss[0, 0] / (2.0 * groups * per_group * full)
    return (mean_loss, query_grad, passage_grad)


def solution(mesh):
    in_specs = (P("dp", "inner", None), P("dp", "inner", None), P())
    out_specs = (P(), P("dp", "inner", None), P("dp", "inner", None))
    return jax.shard_map(body, mesh=mesh, in_specs=in_specs, out_specs=out_specs, check_vma=False)
```

```python
import functools
import math

import jax
import jax.numpy as jnp
from jax import lax
from jax.experimental import pallas as pl
from jax.experimental.pallas import tpu as pltpu
from jax.sharding import PartitionSpec as P

CAP = 2
NEG_FILL = -1e30
LOG2E = math.log2(math.e)
LN2 = math.log(2.0)
ANY = pl.BlockSpec(memory_space=pl.ANY)
SMEM = pl.BlockSpec(memory_space=pltpu.SMEM)
VMEM = pl.BlockSpec(memory_space=pltpu.VMEM)
EXTRA = 16
GROUPED = 3
VMEM_LIMIT = 56 * 1024 * 1024


def slot_tables(neg_lists, groups, per_group, slot_depth):
    block_count = neg_lists.shape[0]
    block_ids = jnp.arange(block_count, dtype=jnp.int32)
    named = jnp.any(neg_lists[:, :, None] == block_ids[None, None, :], axis=1)
    present = jnp.any(named.reshape(groups, per_group, block_count), axis=1)
    present = present.reshape(groups, groups, per_group).astype(jnp.int32)
    slot_ranks = jnp.cumsum(present, axis=2) - 1
    slot_ids = jnp.arange(slot_depth, dtype=jnp.int32)
    hits = (present[..., None] == 1) & (slot_ranks[..., None] == slot_ids[None, None, None, :])
    local_ids = jnp.arange(per_group, dtype=jnp.int32)
    slot_block = jnp.sum(jnp.where(hits, local_ids[None, None, :, None], 0), axis=2)
    slot_live = jnp.any(hits, axis=2)
    return (slot_ranks, slot_block, slot_live)


def join_log2(a, b):
    return jnp.maximum(a, b) + jnp.log2(1.0 + jnp.exp2(-jnp.abs(a - b)))


def row_tile(rows):
    return math.gcd(rows, 256)


def dot_t(a, b):
    return lax.dot_general(a, b, (((1,), (1,)), ((), ())), preferred_element_type=jnp.float32)


def dot_n(a, b):
    return lax.dot_general(a, b, (((0,), (0,)), ((), ())), preferred_element_type=jnp.float32)


def cand_copy(own_p, far_p, slot_ref, picks, block, k, dst, sem):
    rows = own_p.shape[1]
    src = own_p.at[block] if k == 0 else far_p.at[slot_ref[block * picks + k - 1]]
    return pltpu.make_async_copy(src, dst.at[pl.ds(k * rows, rows)], sem)


def query_copies(block, chunk, pos, own_q, from_left, from_right, dst, sems, arrive):
    first, inner = chunk[0], len(from_left) + 1
    rows = own_q.shape[1]

    def piece(src, at, k):
        return pltpu.make_async_copy(src, dst.at[pl.ds(pl.multiple_of(at * rows, rows), rows)], sems.at[k])

    if arrive:
        for k in range(inner):
            piece(own_q.at[block], k, k).wait()
        return
    piece(own_q.at[block], pos, 0).start()
    for k in range(1, inner):
        @pl.when(pos >= k)
        def _():
            piece(from_left[k - 1].at[block - first], pos - k, k).start()

        @pl.when(pos < k)
        def _():
            piece(from_right[inner - k - 1].at[block - first], pos - k + inner, k).start()


def forward_kernel(chunk, inner, picks, scale, *refs):
    pos_ref, slot_ref, id_ref, own_q = refs[:4]
    from_left = refs[4:3 + inner]
    from_right = refs[3 + inner:2 + 2 * inner]
    own_p, far_p, col_in, row_out, col_out, l_out, cands, whole_q, l_buf, sems, q_sems, l_sems = refs[2 + 2 * inner:]
    rows = own_q.shape[1]
    full = rows * inner
    tile = row_tile(full)
    pos = pos_ref[0]
    first, count = chunk

    def cand_copies(b):
        return [
            cand_copy(own_p, far_p, slot_ref, picks, first + b, k, cands.at[b % 2], sems.at[b % 2, k])
            for k in range(picks + 1)
        ]

    def queries(b, arrive):
        query_copies(first + b, chunk, pos, own_q, from_left, from_right, whole_q.at[b % 2], q_sems.at[b % 2], arrive)

    def start(b):
        queries(b, False)
        for copy in cand_copies(b):
            copy.start()

    def keep(b, t):
        part = pl.ds(t * tile, tile)
        return pltpu.make_async_copy(l_buf.at[b, part], l_out.at[b, part], l_sems.at[b, t])

    start(0)
    col_out[...] = col_in[...]
    for b in range(count):
        buf = b % 2
        if b + 1 < count:
            start(b + 1)
        queries(b, True)
        for copy in cand_copies(b):
            copy.wait()
        block_col = None
        for t in range(full // tile):
            logits = dot_t(whole_q[buf, t * tile:(t + 1) * tile, :], cands[buf]) * scale
            l_buf[b, t * tile:(t + 1) * tile] = logits
            keep(b, t).start()
            peak = jnp.max(logits, axis=1, keepdims=True)
            mass = jnp.sum(jnp.exp2(logits - peak), axis=1, keepdims=True)
            row_lse = jnp.broadcast_to(peak + jnp.log2(mass), (tile, 128))
            row_out[b:b + 1, t * tile:(t + 1) * tile] = row_lse.T[0:1, :]
            col_peak = jnp.max(logits, axis=0, keepdims=True)
            col_mass = jnp.sum(jnp.exp2(logits - col_peak), axis=0, keepdims=True)
            col_lse = col_peak + jnp.log2(col_mass)
            block_col = col_lse if block_col is None else join_log2(block_col, col_lse)
        for k in range(picks + 1):
            row = pl.ds(id_ref[(first + b) * (picks + 1) + k], 1)
            col_out[row, :] = join_log2(col_out[row, :], block_col[:, k * rows:(k + 1) * rows])
    for b in range(count):
        for t in range(full // tile):
            keep(b, t).wait()


def scatter_plan(inner):
    if inner == 4:
        return [
            (((0, 1), (3, 2)), {0: 2, 3: 1}, None, False, ()),
            (((2, 0), (1, 3)), {2: 0, 1: 3}, None, True, ()),
            (((2, 1), (1, 2)), {2: 1, 1: 2}, 0, True, ()),
            (((3, 0), (0, 3)), {3: 0, 0: 3}, None, True, (0, 1)),
            (((1, 0), (2, 3)), {1: 0, 2: 3}, None, True, (0, 1)),
            (((0, 1), (3, 2)), {0: 1, 3: 2}, None, True, (0, 1)),
        ]
    plan, place = [], {}
    for m in range(inner - 1):
        for t in range(inner - 1 - m):
            place[(t, m)] = len(plan)
            pairs = ((t, t + 1), (inner - 1 - t, inner - 2 - t))
            sends = {t: inner - 1 - m, inner - 1 - t: m}
            plan.append((pairs, sends, place.get((t - 1, m)), m == inner - 2 - t, ()))
    return plan


def slice_for(pos, sends):
    at = 0
    for device, target in sends.items():
        at = jnp.where(pos == device, target, at)
    return at


def in_pieces(value, width, lane):
    high = value.astype(jnp.bfloat16).astype(jnp.float32)
    mid = (value - high).astype(jnp.bfloat16).astype(jnp.float32)
    low = value - high - mid
    at = lax.broadcasted_iota(jnp.int32, (EXTRA, width), 1) - lane
    pieces = jnp.where(at == 0, high, jnp.where(at == 1, mid, jnp.where(at == 2, low, 0.0)))
    return pieces.astype(jnp.bfloat16)


def query_kernel(plan, chunks, blocks, inner, picks, *refs):
    pos_ref, slot_ref, id_ref, own_p, far_p, row_lse, col_lse = refs[:7]
    l_refs = refs[7:7 + len(chunks)]
    refs = refs[7 + len(chunks):]
    outs = refs[:len(plan) + 1]
    w_out, cands, l_buf, w_buf, dq_buf, piece_buf, sems, l_sems, dq_sems, w_sems = refs[len(plan) + 1:]
    per_group, rows, width = own_p.shape
    full = rows * inner
    tile = row_tile(full)
    pos = pos_ref[0]
    home = {at + n: (c, n) for c, (at, size) in enumerate(chunks) for n in range(size)}

    def incoming(b):
        c, n = home[b]
        return [pltpu.make_async_copy(l_refs[c].at[n], l_buf.at[b % 2], l_sems.at[b % 2])] + [
            cand_copy(own_p, far_p, slot_ref, picks, b, k, cands.at[b % 2], sems.at[b % 2, k])
            for k in range(picks + 1)
        ]

    def w_copy(b, t):
        part = pl.ds(t * tile, tile)
        return pltpu.make_async_copy(w_buf.at[b, part], w_out.at[b, part], w_sems.at[b, t])

    def outgoing(b, act):
        for n, out in enumerate(outs):
            sends = plan[n][1] if n < len(plan) else {d: d for d in range(inner)}

            @pl.when(functools.reduce(jnp.logical_or, [pos == d for d in sends]))
            def _():
                if b < per_group:
                    at = pl.multiple_of(slice_for(pos, sends) * rows, rows)
                    src, dst = dq_buf.at[b, pl.ds(at, rows)], out.at[pl.ds(b * rows, rows)]
                else:
                    src, dst = piece_buf, out.at[pl.ds(per_group * rows, EXTRA)]
                copy = pltpu.make_async_copy(src, dst, dq_sems.at[b, n])
                copy.wait() if act == "wait" else copy.start()

    for copy in incoming(0):
        copy.start()
    loss_cols = jnp.sum(col_lse[0:blocks, :]) * LN2 - 2.0 * jnp.sum(col_lse[blocks:blocks + 1, 0:1])
    piece_buf[...] = in_pieces(loss_cols, width, 3 * pos)
    outgoing(per_group, "start")
    for b in range(per_group):
        buf = b % 2
        if b + 1 < per_group:
            for copy in incoming(b + 1):
                copy.start()
        col = jnp.concatenate(
            [col_lse[pl.ds(id_ref[b * (picks + 1) + k], 1), :] for k in range(picks + 1)], axis=1
        ) + 1.0
        row = jnp.broadcast_to(row_lse[b:b + 1, :] + 1.0, (128, full)).T
        for copy in incoming(b):
            copy.wait()
        for t in range(full // tile):
            part = slice(t * tile, (t + 1) * tile)
            logits = l_buf[buf, part, :]
            probs = jnp.exp2(logits - row[part, 0:1]) + jnp.exp2(logits - col)
            r_id = lax.broadcasted_iota(jnp.int32, (tile, rows), 0) + t * tile - pos * rows
            c_id = lax.broadcasted_iota(jnp.int32, (tile, rows), 1)
            target = jnp.where(r_id == c_id, 1.0, 0.0)
            w_buf[b, part, 0:rows] = (probs[:, 0:rows] - target).astype(jnp.bfloat16)
            w_buf[b, part, rows:] = probs[:, rows:].astype(jnp.bfloat16)
            w_copy(b, t).start()
            grad = jnp.dot(w_buf[b, part, :], cands[buf], preferred_element_type=jnp.float32)
            dq_buf[b, part] = grad.astype(jnp.bfloat16)
        outgoing(b, "start")
    for b in range(per_group + 1):
        outgoing(b, "wait")
    for b in range(per_group):
        for t in range(full // tile):
            w_copy(b, t).wait()


def passage_kernel(chunks, inner, picks, *refs):
    pos_ref, slot_ref, own_q = refs[:3]
    place = 3
    rings = []
    for _ in chunks:
        rings.append((refs[place:place + inner - 1], refs[place + inner - 1:place + 2 * inner - 2]))
        place += 2 * inner - 2
    w_in, row_lse, own_out, far_out, whole_q, w_buf, own_acc, far_acc, far_buf, q_sems, w_sems, far_sems = refs[place:]
    per_group, rows, width = own_q.shape
    groups, packed = far_buf.shape[:2]
    depth = packed // rows
    pos = pos_ref[0]
    home = {at + n: c for c, (at, size) in enumerate(chunks) for n in range(size)}

    def queries(b, arrive):
        c = home[b]
        query_copies(b, chunks[c], pos, own_q, *rings[c], whole_q.at[b % 2], q_sems.at[b % 2], arrive)

    def w_copy(b):
        return pltpu.make_async_copy(w_in.at[b], w_buf.at[b % 2], w_sems.at[b % 2])

    def own_copy(b):
        return pltpu.make_async_copy(own_acc.at[b], own_out.at[b], far_sems.at[groups + b])

    queries(0, False)
    w_copy(0).start()
    far_acc[...] = jnp.zeros_like(far_acc)
    for b in range(per_group):
        buf = b % 2
        if b + 1 < per_group:
            queries(b + 1, False)
            w_copy(b + 1).start()
        queries(b, True)
        w_copy(b).wait()
        step = math.gcd(picks + 1, GROUPED)
        for k in range(0, picks + 1, step):
            parts = dot_n(w_buf[buf, :, k * rows:(k + step) * rows], whole_q[buf])
            for j in range(step):
                part = parts[j * rows:(j + 1) * rows]
                if k + j == 0:
                    own_acc[b] = part
                    own_copy(b).start()
                else:
                    slot = slot_ref[b * picks + k + j - 1]
                    far_acc[slot] = far_acc[slot] + part
    row_pieces = in_pieces(jnp.sum(row_lse[0:per_group, :]) * LN2, width, 0)
    for g in range(groups):
        for c in range(depth):
            far_buf[g, c * rows:(c + 1) * rows] = far_acc[g * depth + c].astype(jnp.bfloat16)
        far_buf[g, depth * rows:] = row_pieces
        pltpu.make_async_copy(far_buf.at[g], far_out.at[g], far_sems.at[g]).start()
    for g in range(groups):
        pltpu.make_async_copy(far_buf.at[g], far_out.at[g], far_sems.at[g]).wait()
    for b in range(per_group):
        own_copy(b).wait()


def finish_kernel(depth, dest_ref, own_ref, far_ref, out_ref, loss_ref, acc, got, sems):
    groups = far_ref.shape[0]
    per_group, rows, _ = out_ref.shape

    def copy(g):
        return pltpu.make_async_copy(far_ref.at[g], got.at[g], sems.at[g])

    own = pltpu.make_async_copy(own_ref, acc.at[pl.ds(0, per_group)], sems.at[groups])
    own.start()
    for g in range(groups):
        copy(g).start()
    own.wait()
    pieces = None
    for g in range(groups):
        copy(g).wait()
        for c in range(depth):
            dest = dest_ref[g * depth + c]
            acc[dest] = acc[dest] + got[g, c * rows:(c + 1) * rows].astype(jnp.float32)
        row = got[g, depth * rows:, 0:128].astype(jnp.float32)
        pieces = row if pieces is None else pieces + row
    loss_ref[...] = jnp.sum(pieces[0:8], axis=1, keepdims=True) + jnp.zeros((8, 128), jnp.float32)
    out_ref[...] = acc[0:per_group].astype(jnp.bfloat16)


def after(value, *events):
    return lax.optimization_barrier((value, *events))[0]


def doublings(size):
    return [1 << n for n in range(size.bit_length() - 1)]


def butterfly(value, axis, size, join):
    for step in doublings(size):
        other = lax.ppermute(value, axis, [(i, i ^ step) for i in range(size)])
        value = join(value, other)
    return value


def body(queries, passages, neg_lists):
    per_group, rows, width = queries.shape
    picks = neg_lists.shape[1]
    blocks = neg_lists.shape[0]
    groups = lax.axis_size("dp")
    inner = lax.axis_size("inner")
    full = rows * inner
    cand_rows = (picks + 1) * rows
    slot_count = groups * CAP
    scale = 1.0 / math.sqrt(width)
    my_group = lax.axis_index("dp")
    pos = lax.axis_index("inner")
    f32, bf16 = jnp.float32, jnp.bfloat16
    params = pltpu.CompilerParams(vmem_limit_bytes=VMEM_LIMIT)
    block_flops = 2 * full * cand_rows * width
    block_bytes = 2 * (full + cand_rows) * width

    def cost(blocks, products):
        return pl.CostEstimate(
            flops=blocks * products * block_flops, bytes_accessed=blocks * products * block_bytes, transcendentals=0
        )

    half = per_group // 2
    chunks = [(0, half), (half, per_group - half)]
    lefts = [[] for _ in chunks]
    rights = [[] for _ in chunks]
    moving = [[queries[at:at + size]] * 2 for at, size in chunks]
    for s in range(1, inner):
        for c in range(len(chunks)):
            moving[c] = [
                lax.ppermute(moving[c][0], "inner", [(i, i + 1) for i in range(s - 1, inner - 1)]),
                lax.ppermute(moving[c][1], "inner", [(i, i - 1) for i in range(inner - s, 0, -1)]),
            ]
            lefts[c].append(moving[c][0])
            rights[c].append(moving[c][1])

    slot_ranks, slot_block, slot_live = slot_tables(neg_lists, groups, per_group, CAP)
    listed = lax.dynamic_slice_in_dim(neg_lists, my_group * per_group, per_group, 0)
    my_ranks = lax.dynamic_index_in_dim(slot_ranks, my_group, 0, keepdims=False)
    slot_of = (listed // per_group) * CAP + my_ranks[listed // per_group, listed % per_group]
    slot_flat = slot_of.reshape(-1)
    own_ids = my_group * per_group + jnp.arange(per_group, dtype=jnp.int32)
    id_flat = jnp.concatenate([own_ids[:, None], listed], axis=1).reshape(-1)
    pos_arr = pos.reshape(1)
    sends_for = lax.dynamic_index_in_dim(slot_block, my_group, 1, keepdims=False)
    live_for = lax.dynamic_index_in_dim(slot_live, my_group, 1, keepdims=False)
    outgoing = passages[sends_for]
    arrived = lax.all_to_all(outgoing, "dp", split_axis=0, concat_axis=0, tiled=True)
    arrived = arrived.reshape(slot_count, rows, width)

    fetch_scratch = [
        pltpu.VMEM((2, cand_rows, width), bf16),
        pltpu.VMEM((2, full, width), bf16),
    ]
    fetch_sems = [pltpu.SemaphoreType.DMA((2, picks + 1)), pltpu.SemaphoreType.DMA((2, inner))]
    own_sum = jnp.sum(queries.astype(f32) * passages.astype(f32)) * scale
    col = jnp.concatenate([jnp.full((blocks, rows), NEG_FILL, f32), jnp.broadcast_to(own_sum, (8, rows))])
    row_parts, logits = [], []
    tiles = full // row_tile(full)
    for c, chunk in enumerate(chunks):
        row_part, col, logit = pl.pallas_call(
            functools.partial(forward_kernel, chunk, inner, picks, scale * LOG2E),
            out_shape=(
                jax.ShapeDtypeStruct((chunk[1], full), f32),
                jax.ShapeDtypeStruct(col.shape, f32),
                jax.ShapeDtypeStruct((chunk[1], full, cand_rows), f32),
            ),
            in_specs=[SMEM] * 3 + [ANY] * (2 * inner + 1) + [VMEM],
            out_specs=(VMEM, VMEM, ANY),
            scratch_shapes=fetch_scratch + [pltpu.VMEM((chunk[1], full, cand_rows), f32)] + fetch_sems + [
                pltpu.SemaphoreType.DMA((chunk[1], tiles))
            ],
            compiler_params=params,
            cost_estimate=cost(chunk[1], 1),
            name=f"forward_{c}",
        )(pos_arr, slot_flat, id_flat, queries, *lefts[c], *rights[c], passages, arrived, col)
        row_parts.append(row_part)
        logits.append(logit)
    row = jnp.concatenate(row_parts, axis=0)
    is_lse = jnp.arange(blocks + 8)[:, None] < blocks
    col_lse = butterfly(col, "dp", groups, lambda a, b: jnp.where(is_lse, join_log2(a, b), a + b))
    row_lse = butterfly(row, "inner", inner, join_log2)

    packed = CAP * rows + EXTRA
    flat = per_group * rows + EXTRA
    plan = scatter_plan(inner)
    *parts, weights = pl.pallas_call(
        functools.partial(query_kernel, plan, chunks, blocks, inner, picks),
        out_shape=(jax.ShapeDtypeStruct((flat, width), bf16),) * (len(plan) + 1)
        + (jax.ShapeDtypeStruct((per_group, full, cand_rows), bf16),),
        in_specs=[SMEM] * 3 + [ANY] * 2 + [VMEM] * 2 + [ANY] * len(chunks),
        out_specs=(ANY,) * (len(plan) + 2),
        scratch_shapes=[
            pltpu.VMEM((2, cand_rows, width), bf16),
            pltpu.VMEM((2, full, cand_rows), f32),
            pltpu.VMEM((per_group, full, cand_rows), bf16),
            pltpu.VMEM((per_group, full, width), bf16),
            pltpu.VMEM((EXTRA, width), bf16),
            pltpu.SemaphoreType.DMA((2, picks + 1)),
            pltpu.SemaphoreType.DMA((2,)),
            pltpu.SemaphoreType.DMA((per_group + 1, len(plan) + 1)),
            pltpu.SemaphoreType.DMA((per_group, tiles)),
        ],
        compiler_params=params,
        cost_estimate=cost(per_group, 1),
        name="query",
    )(pos_arr, slot_flat, id_flat, passages, arrived, row_lse, col_lse, *logits)

    rings = []
    for c in range(len(chunks)):
        rings += [*lefts[c], *rights[c]]
    own_grad, far_grad = pl.pallas_call(
        functools.partial(passage_kernel, chunks, inner, picks),
        out_shape=(
            jax.ShapeDtypeStruct((per_group, rows, width), f32),
            jax.ShapeDtypeStruct((groups, packed, width), bf16),
        ),
        in_specs=[SMEM] * 2 + [ANY] * (2 + len(rings)) + [VMEM],
        out_specs=(ANY, ANY),
        scratch_shapes=[
            pltpu.VMEM((2, full, width), bf16),
            pltpu.VMEM((2, full, cand_rows), bf16),
            pltpu.VMEM((per_group, rows, width), f32),
            pltpu.VMEM((slot_count, rows, width), f32),
            pltpu.VMEM((groups, packed, width), bf16),
            pltpu.SemaphoreType.DMA((2, inner)),
            pltpu.SemaphoreType.DMA((2,)),
            pltpu.SemaphoreType.DMA((groups + per_group,)),
        ],
        compiler_params=params,
        cost_estimate=cost(per_group, 1),
        name="passage",
    )(pos_arr, slot_flat, queries, *rings, weights, row_lse)

    sums = []
    query_sum = parts[-1].astype(f32)
    for n, (pairs, sends, adds, final, gates) in enumerate(plan):
        out = parts[n]
        if adds is not None:
            out = (out.astype(f32) + sums[adds]).astype(bf16)
        if gates:
            out = after(out, *[sums[g] for g in gates])
        sums.append(lax.ppermute(out, "inner", pairs))
        if final:
            query_sum = query_sum + sums[-1]
    loss_cols = jnp.sum(query_sum[per_group * rows, :3 * inner])
    query_grad = query_sum[:per_group * rows].astype(bf16).reshape(per_group, rows, width)

    far_grad = after(far_grad, *sums[:2])
    returned = lax.all_to_all(far_grad, "dp", split_axis=0, concat_axis=0, tiled=True)
    dest = jnp.where(live_for, sends_for, per_group).reshape(-1)
    passage_grad, total = pl.pallas_call(
        functools.partial(finish_kernel, CAP),
        out_shape=(
            jax.ShapeDtypeStruct((per_group, rows, width), bf16),
            jax.ShapeDtypeStruct((8, 128), f32),
        ),
        in_specs=[SMEM, ANY, ANY],
        out_specs=(VMEM, VMEM),
        scratch_shapes=[
            pltpu.VMEM((per_group + 1, rows, width), f32),
            pltpu.VMEM((groups, packed, width), bf16),
            pltpu.SemaphoreType.DMA((groups + 1,)),
        ],
        compiler_params=params,
        name="finish",
    )(dest, own_grad, returned)
    mean_loss = (total[0, 0] + loss_cols) / (2.0 * groups * per_group * full)
    return (mean_loss, query_grad, passage_grad)


def solution(mesh):
    in_specs = (P("dp", "inner", None), P("dp", "inner", None), P())
    out_specs = (P(), P("dp", "inner", None), P("dp", "inner", None))
    return jax.shard_map(body, mesh=mesh, in_specs=in_specs, out_specs=out_specs, check_vma=False)
```

```python
import functools
import math

import jax
import jax.numpy as jnp
from jax import lax
from jax.experimental import pallas as pl
from jax.experimental.pallas import tpu as pltpu
from jax.sharding import PartitionSpec as P

CAP = 2
NEG_FILL = -1e30
LOG2E = math.log2(math.e)
LN2 = math.log(2.0)
ANY = pl.BlockSpec(memory_space=pl.ANY)
SMEM = pl.BlockSpec(memory_space=pltpu.SMEM)
VMEM = pl.BlockSpec(memory_space=pltpu.VMEM)
EXTRA = 16
GROUPED = 3
MIB = 1024 * 1024


def slot_tables(neg_lists, groups, per_group, slot_depth):
    block_count = neg_lists.shape[0]
    block_ids = jnp.arange(block_count, dtype=jnp.int32)
    named = jnp.any(neg_lists[:, :, None] == block_ids[None, None, :], axis=1)
    present = jnp.any(named.reshape(groups, per_group, block_count), axis=1)
    present = present.reshape(groups, groups, per_group).astype(jnp.int32)
    slot_ranks = jnp.cumsum(present, axis=2) - 1
    slot_ids = jnp.arange(slot_depth, dtype=jnp.int32)
    hits = (present[..., None] == 1) & (slot_ranks[..., None] == slot_ids[None, None, None, :])
    local_ids = jnp.arange(per_group, dtype=jnp.int32)
    slot_block = jnp.sum(jnp.where(hits, local_ids[None, None, :, None], 0), axis=2)
    slot_live = jnp.any(hits, axis=2)
    return (slot_ranks, slot_block, slot_live)


def join_log2(a, b):
    return jnp.maximum(a, b) + jnp.log2(1.0 + jnp.exp2(-jnp.abs(a - b)))


def row_tile(rows):
    return math.gcd(rows, 256)


def dot_t(a, b):
    return lax.dot_general(a, b, (((1,), (1,)), ((), ())), preferred_element_type=jnp.float32)


def dot_n(a, b):
    return lax.dot_general(a, b, (((0,), (0,)), ((), ())), preferred_element_type=jnp.float32)


def cand_copy(own_p, far_p, slot_ref, picks, block, k, dst, sem):
    rows = own_p.shape[1]
    src = own_p.at[block] if k == 0 else far_p.at[slot_ref[block * picks + k - 1]]
    return pltpu.make_async_copy(src, dst.at[pl.ds(k * rows, rows)], sem)


def query_copies(block, chunk, pos, own_q, from_left, from_right, dst, sems, arrive):
    first, inner = chunk[0], len(from_left) + 1
    rows = own_q.shape[1]

    def piece(src, at, k):
        return pltpu.make_async_copy(src, dst.at[pl.ds(pl.multiple_of(at * rows, rows), rows)], sems.at[k])

    if arrive:
        for k in range(inner):
            piece(own_q.at[block], k, k).wait()
        return
    piece(own_q.at[block], pos, 0).start()
    for k in range(1, inner):
        @pl.when(pos >= k)
        def _():
            piece(from_left[k - 1].at[block - first], pos - k, k).start()

        @pl.when(pos < k)
        def _():
            piece(from_right[inner - k - 1].at[block - first], pos - k + inner, k).start()


def collect_kernel(picks, slot_ref, own_p, far_p, cands, sems):
    copies = [
        cand_copy(own_p, far_p, slot_ref, picks, b, k, cands.at[b], sems.at[b, k])
        for b in range(cands.shape[0])
        for k in range(picks + 1)
    ]
    for copy in copies:
        copy.start()
    for copy in copies:
        copy.wait()


def forward_kernel(chunk, inner, picks, scale, *refs):
    pos_ref, id_ref, own_q = refs[:3]
    from_left = refs[3:2 + inner]
    from_right = refs[2 + inner:1 + 2 * inner]
    cands, col_in, row_out, col_out, l_out, whole_q, q_sems = refs[1 + 2 * inner:]
    rows = own_q.shape[1]
    full = rows * inner
    tile = row_tile(full)
    pos = pos_ref[0]
    first, count = chunk

    def queries(b, arrive):
        query_copies(first + b, chunk, pos, own_q, from_left, from_right, whole_q.at[b], q_sems.at[b], arrive)

    for b in range(count):
        queries(b, False)
    col_out[...] = col_in[...]
    for b in range(count):
        queries(b, True)
        block_col = None
        for t in range(full // tile):
            logits = dot_t(whole_q[b, t * tile:(t + 1) * tile, :], cands[first + b]) * scale
            l_out[b, t * tile:(t + 1) * tile] = logits
            peak = jnp.max(logits, axis=1, keepdims=True)
            mass = jnp.sum(jnp.exp2(logits - peak), axis=1, keepdims=True)
            row_lse = jnp.broadcast_to(peak + jnp.log2(mass), (tile, 128))
            row_out[b:b + 1, t * tile:(t + 1) * tile] = row_lse.T[0:1, :]
            col_peak = jnp.max(logits, axis=0, keepdims=True)
            col_mass = jnp.sum(jnp.exp2(logits - col_peak), axis=0, keepdims=True)
            col_lse = col_peak + jnp.log2(col_mass)
            block_col = col_lse if block_col is None else join_log2(block_col, col_lse)
        for k in range(picks + 1):
            row = pl.ds(id_ref[(first + b) * (picks + 1) + k], 1)
            col_out[row, :] = join_log2(col_out[row, :], block_col[:, k * rows:(k + 1) * rows])


def scatter_plan(inner):
    if inner == 4:
        return [
            (((0, 1), (3, 2), (2, 0), (1, 3)), {0: 2, 3: 1, 2: 0, 1: 3}, None, (), (0, 3)),
            (((2, 1), (1, 2), (3, 0), (0, 3)), {2: 1, 1: 2, 3: 0, 0: 3}, (0, (1, 2)), (0,), (0, 1, 2, 3)),
            (((0, 1), (1, 0), (2, 3), (3, 2)), {0: 1, 1: 0, 2: 3, 3: 2}, None, (0,), (0, 1, 2, 3)),
        ]
    plan, place = [], {}
    for m in range(inner - 1):
        for t in range(inner - 1 - m):
            place[(t, m)] = len(plan)
            pairs = ((t, t + 1), (inner - 1 - t, inner - 2 - t))
            sends = {t: inner - 1 - m, inner - 1 - t: m}
            adds = (place[(t - 1, m)], tuple(sends)) if t else None
            plan.append((pairs, sends, adds, (), (t + 1, inner - 2 - t) if m == inner - 2 - t else ()))
    return plan


def one_of(pos, devices):
    return functools.reduce(jnp.logical_or, [pos == d for d in devices])


def slice_for(pos, sends):
    at = 0
    for device, target in sends.items():
        at = jnp.where(pos == device, target, at)
    return at


def in_pieces(value, width, lane):
    high = value.astype(jnp.bfloat16).astype(jnp.float32)
    mid = (value - high).astype(jnp.bfloat16).astype(jnp.float32)
    low = value - high - mid
    at = lax.broadcasted_iota(jnp.int32, (EXTRA, width), 1) - lane
    pieces = jnp.where(at == 0, high, jnp.where(at == 1, mid, jnp.where(at == 2, low, 0.0)))
    return pieces.astype(jnp.bfloat16)


def column_lse(b, picks, id_ref, col_lse):
    return jnp.concatenate(
        [col_lse[pl.ds(id_ref[b * (picks + 1) + k], 1), :] for k in range(picks + 1)], axis=1
    ) + 1.0


def block_weights(logits, row, col, first_row, rows, w_ref):
    probs = jnp.exp2(logits - row) + jnp.exp2(logits - col)
    r_id = lax.broadcasted_iota(jnp.int32, (logits.shape[0], rows), 0) + first_row
    c_id = lax.broadcasted_iota(jnp.int32, (logits.shape[0], rows), 1)
    target = jnp.where(r_id == c_id, 1.0, 0.0)
    w_ref[:, 0:rows] = (probs[:, 0:rows] - target).astype(jnp.bfloat16)
    w_ref[:, rows:] = probs[:, rows:].astype(jnp.bfloat16)


def loss_piece(blocks, pos, col_lse, width):
    value = jnp.sum(col_lse[0:blocks, :]) * LN2 - 2.0 * jnp.sum(col_lse[blocks:blocks + 1, 0:1])
    return in_pieces(value, width, 3 * pos)


def early_kernel(sends, chunks, blocks, inner, picks, *refs):
    pos_ref, id_ref, cands, row_lse, col_lse = refs[:5]
    l_refs = refs[5:5 + len(chunks)]
    out, w_buf, row_buf, dq_buf, sems = refs[5 + len(chunks):]
    per_group, full = row_lse.shape
    rows = full // inner
    width = out.shape[1]
    pos = pos_ref[0]
    at = slice_for(pos, sends)
    start = pl.multiple_of(at * rows, rows)
    home = {first + n: (c, n) for c, (first, size) in enumerate(chunks) for n in range(size)}
    dq_buf[per_group * rows:] = loss_piece(blocks, pos, col_lse, width)

    def copy(b):
        part = pl.ds(b * rows, rows if b < per_group else EXTRA)
        return pltpu.make_async_copy(dq_buf.at[part], out.at[part], sems.at[b])

    copy(per_group).start()
    for b in range(per_group):
        c, n = home[b]
        row_buf[...] = jnp.broadcast_to(row_lse[b:b + 1, :] + 1.0, (128, full)).T
        block_weights(
            l_refs[c][n, pl.ds(start, rows), :], row_buf[pl.ds(start, rows), 0:1],
            column_lse(b, picks, id_ref, col_lse), (at - pos) * rows, rows, w_buf.at[b],
        )
        grad = jnp.dot(w_buf[b], cands[b], preferred_element_type=jnp.float32)
        dq_buf[b * rows:(b + 1) * rows] = grad.astype(jnp.bfloat16)
        copy(b).start()
    for b in range(per_group + 1):
        copy(b).wait()


def query_kernel(out_slices, chunks, blocks, inner, picks, *refs):
    pos_ref, id_ref, cands, row_lse, col_lse = refs[:5]
    l_refs = refs[5:5 + len(chunks)]
    refs = refs[5 + len(chunks):]
    outs = refs[:len(out_slices)]
    w_buf, dq_buf, piece_buf, dq_sems = refs[len(out_slices):]
    per_group, full, width = dq_buf.shape
    rows = full // inner
    tile = row_tile(full)
    pos = pos_ref[0]
    home = {at + n: (c, n) for c, (at, size) in enumerate(chunks) for n in range(size)}

    def outgoing(b, act):
        for n, (out, sends) in enumerate(zip(outs, out_slices)):
            @pl.when(one_of(pos, sends))
            def _():
                if b < per_group:
                    at = pl.multiple_of(slice_for(pos, sends) * rows, rows)
                    src, dst = dq_buf.at[b, pl.ds(at, rows)], out.at[pl.ds(b * rows, rows)]
                else:
                    src, dst = piece_buf, out.at[pl.ds(per_group * rows, EXTRA)]
                copy = pltpu.make_async_copy(src, dst, dq_sems.at[b, n])
                copy.wait() if act == "wait" else copy.start()

    piece_buf[...] = loss_piece(blocks, pos, col_lse, width)
    outgoing(per_group, "start")
    for b in range(per_group):
        c, n = home[b]
        col = column_lse(b, picks, id_ref, col_lse)
        row = jnp.broadcast_to(row_lse[b:b + 1, :] + 1.0, (128, full)).T
        for t in range(full // tile):
            part = slice(t * tile, (t + 1) * tile)
            block_weights(
                l_refs[c][n, part, :], row[part, 0:1], col, t * tile - pos * rows, rows, w_buf.at[b, part]
            )
            grad = jnp.dot(w_buf[b, part, :], cands[b], preferred_element_type=jnp.float32)
            dq_buf[b, part] = grad.astype(jnp.bfloat16)
        outgoing(b, "start")
    for b in range(per_group + 1):
        outgoing(b, "wait")


def passage_kernel(chunks, picks, *refs):
    slot_ref, row_lse, weights = refs[:3]
    q_refs = refs[3:3 + len(chunks)]
    own_out, far_out, own_acc, far_acc, far_buf, far_sems = refs[3 + len(chunks):]
    per_group, rows, width = own_acc.shape
    groups, packed = far_buf.shape[:2]
    depth = packed // rows
    home = {at + n: (c, n) for c, (at, size) in enumerate(chunks) for n in range(size)}

    def own_copy(b):
        return pltpu.make_async_copy(own_acc.at[b], own_out.at[b], far_sems.at[groups + b])

    far_acc[...] = jnp.zeros_like(far_acc)
    for b in range(per_group):
        c, n = home[b]
        step = math.gcd(picks + 1, GROUPED)
        for k in range(0, picks + 1, step):
            parts = dot_n(weights[b, :, k * rows:(k + step) * rows], q_refs[c][n])
            for j in range(step):
                part = parts[j * rows:(j + 1) * rows]
                if k + j == 0:
                    own_acc[b] = part
                    own_copy(b).start()
                else:
                    slot = slot_ref[b * picks + k + j - 1]
                    far_acc[slot] = far_acc[slot] + part
    row_pieces = in_pieces(jnp.sum(row_lse[0:per_group, :]) * LN2, width, 0)
    for g in range(groups):
        for c in range(depth):
            far_buf[g, c * rows:(c + 1) * rows] = far_acc[g * depth + c].astype(jnp.bfloat16)
        far_buf[g, depth * rows:] = row_pieces
        pltpu.make_async_copy(far_buf.at[g], far_out.at[g], far_sems.at[g]).start()
    for g in range(groups):
        pltpu.make_async_copy(far_buf.at[g], far_out.at[g], far_sems.at[g]).wait()
    for b in range(per_group):
        own_copy(b).wait()


def finish_kernel(depth, inner, finals, pos_ref, dest_ref, mine_ref, own_ref, far_ref, *refs):
    moved = refs[:len(finals)]
    q_out, p_out, loss_ref, acc, got, q_got, sems, q_sems = refs[len(finals):]
    groups = far_ref.shape[0]
    per_group, rows, _ = p_out.shape
    pos = pos_ref[0]

    def far_copy(g):
        return pltpu.make_async_copy(far_ref.at[g], got.at[g], sems.at[g])

    def moved_copy(n):
        return pltpu.make_async_copy(moved[n], q_got.at[n], q_sems.at[n])

    for n, devices in enumerate(finals):
        @pl.when(one_of(pos, devices))
        def _():
            moved_copy(n).start()
    for g in range(groups):
        far_copy(g).start()
    ends = {}
    for d in range(inner):
        ends.setdefault(tuple(n for n, devices in enumerate(finals) if d in devices), []).append(d)
    lane = lax.broadcasted_iota(jnp.int32, (8, 128), 1)
    for which, devices in ends.items():
        @pl.when(one_of(pos, devices))
        def _():
            for n in which:
                moved_copy(n).wait()
            for b in range(per_group):
                part = slice(b * rows, (b + 1) * rows)
                value = mine_ref[part, :].astype(jnp.float32)
                for n in which:
                    value = value + q_got[n, part, :].astype(jnp.float32)
                q_out[b] = value.astype(jnp.bfloat16)
            piece = mine_ref[per_group * rows:, 0:128].astype(jnp.float32)
            for n in which:
                piece = piece + q_got[n, per_group * rows:, 0:128].astype(jnp.float32)
            loss_ref[...] = jnp.where(lane < 3 * inner, piece[0:8], 0.0)
    acc[0:per_group] = own_ref[...]
    pieces = loss_ref[...]
    for g in range(groups):
        far_copy(g).wait()
        for c in range(depth):
            dest = dest_ref[g * depth + c]
            acc[dest] = acc[dest] + got[g, c * rows:(c + 1) * rows].astype(jnp.float32)
        pieces = pieces + got[g, depth * rows:, 0:128].astype(jnp.float32)[0:8]
    loss_ref[...] = jnp.sum(pieces, axis=1, keepdims=True) + jnp.zeros((8, 128), jnp.float32)
    p_out[...] = acc[0:per_group].astype(jnp.bfloat16)


def after(value, *events):
    return lax.optimization_barrier((value, *events))[0]


def doublings(size):
    return [1 << n for n in range(size.bit_length() - 1)]


def butterfly(value, axis, size, join):
    for step in doublings(size):
        other = lax.ppermute(value, axis, [(i, i ^ step) for i in range(size)])
        value = join(value, other)
    return value


def body(queries, passages, neg_lists):
    per_group, rows, width = queries.shape
    picks = neg_lists.shape[1]
    blocks = neg_lists.shape[0]
    groups = lax.axis_size("dp")
    inner = lax.axis_size("inner")
    full = rows * inner
    cand_rows = (picks + 1) * rows
    slot_count = groups * CAP
    scale = 1.0 / math.sqrt(width)
    my_group = lax.axis_index("dp")
    pos = lax.axis_index("inner")
    f32, bf16 = jnp.float32, jnp.bfloat16

    def params(mib):
        return pltpu.CompilerParams(vmem_limit_bytes=mib * MIB)

    def in_hbm(*shape):
        return pltpu.HBM(shape, bf16)

    def resident(value):
        return pltpu.with_memory_space_constraint(value, pltpu.VMEM)

    block_flops = 2 * full * cand_rows * width
    block_bytes = 2 * (full + cand_rows) * width

    def cost(blocks, products):
        return pl.CostEstimate(
            flops=blocks * products * block_flops, bytes_accessed=blocks * products * block_bytes, transcendentals=0
        )

    half = per_group // 2
    chunks = [(0, half), (half, per_group - half)]
    lefts = [[] for _ in chunks]
    rights = [[] for _ in chunks]
    moving = [[queries[at:at + size]] * 2 for at, size in chunks]
    for s in range(1, inner):
        for c in range(len(chunks)):
            moving[c] = [
                lax.ppermute(moving[c][0], "inner", [(i, i + 1) for i in range(s - 1, inner - 1)]),
                lax.ppermute(moving[c][1], "inner", [(i, i - 1) for i in range(inner - s, 0, -1)]),
            ]
            lefts[c].append(moving[c][0])
            rights[c].append(moving[c][1])

    slot_ranks, slot_block, slot_live = slot_tables(neg_lists, groups, per_group, CAP)
    listed = lax.dynamic_slice_in_dim(neg_lists, my_group * per_group, per_group, 0)
    my_ranks = lax.dynamic_index_in_dim(slot_ranks, my_group, 0, keepdims=False)
    slot_of = (listed // per_group) * CAP + my_ranks[listed // per_group, listed % per_group]
    slot_flat = slot_of.reshape(-1)
    own_ids = my_group * per_group + jnp.arange(per_group, dtype=jnp.int32)
    id_flat = jnp.concatenate([own_ids[:, None], listed], axis=1).reshape(-1)
    pos_arr = pos.reshape(1)
    sends_for = lax.dynamic_index_in_dim(slot_block, my_group, 1, keepdims=False)
    live_for = lax.dynamic_index_in_dim(slot_live, my_group, 1, keepdims=False)
    outgoing = passages[sends_for]
    arrived = lax.all_to_all(outgoing, "dp", split_axis=0, concat_axis=0, tiled=True)
    arrived = arrived.reshape(slot_count, rows, width)

    own_sum = jnp.sum(queries.astype(f32) * passages.astype(f32)) * scale
    col = jnp.concatenate([jnp.full((blocks, rows), NEG_FILL, f32), jnp.broadcast_to(own_sum, (8, rows))])
    cands = pl.pallas_call(
        functools.partial(collect_kernel, picks),
        out_shape=pltpu.VMEM((per_group, cand_rows, width), bf16),
        in_specs=[SMEM, ANY, ANY],
        out_specs=VMEM,
        scratch_shapes=[pltpu.SemaphoreType.DMA((per_group, picks + 1))],
        compiler_params=params(2),
        name="collect",
    )(slot_flat, passages, arrived)
    cands = resident(cands)
    row_parts, logits, wholes = [], [], []
    for c, chunk in enumerate(chunks):
        row_part, col, logit, whole = pl.pallas_call(
            functools.partial(forward_kernel, chunk, inner, picks, scale * LOG2E),
            out_shape=(
                jax.ShapeDtypeStruct((chunk[1], full), f32),
                jax.ShapeDtypeStruct(col.shape, f32),
                pltpu.VMEM((chunk[1], full, cand_rows), f32),
                pltpu.VMEM((chunk[1], full, width), bf16),
            ),
            in_specs=[SMEM] * 2 + [ANY] * (2 * inner - 1) + [VMEM] * 2,
            out_specs=(VMEM,) * 4,
            scratch_shapes=[pltpu.SemaphoreType.DMA((chunk[1], inner))],
            compiler_params=params(12),
            cost_estimate=cost(chunk[1], 1),
            name=f"forward_{c}",
        )(pos_arr, id_flat, queries, *lefts[c], *rights[c], cands, col)
        row_parts.append(row_part)
        logits.append(resident(logit))
        wholes.append(resident(whole))
    row = jnp.concatenate(row_parts, axis=0)
    is_lse = jnp.arange(blocks + 8)[:, None] < blocks
    col_lse = butterfly(col, "dp", groups, lambda a, b: jnp.where(is_lse, join_log2(a, b), a + b))
    row_lse = butterfly(row, "inner", inner, join_log2)

    packed = CAP * rows + EXTRA
    flat = per_group * rows + EXTRA
    plan = scatter_plan(inner)
    first = pl.pallas_call(
        functools.partial(early_kernel, plan[0][1], chunks, blocks, inner, picks),
        out_shape=in_hbm(flat, width),
        in_specs=[SMEM] * 2 + [VMEM] * (3 + len(chunks)),
        out_specs=ANY,
        scratch_shapes=[
            pltpu.VMEM((per_group, rows, cand_rows), bf16),
            pltpu.VMEM((full, 128), f32),
            pltpu.VMEM((flat, width), bf16),
            pltpu.SemaphoreType.DMA((per_group + 1,)),
        ],
        compiler_params=params(12),
        cost_estimate=cost(1, 1),
        name="early",
    )(pos_arr, id_flat, cands, row_lse, col_lse, *logits)
    own_slice = {d: d for d in range(inner)}
    out_slices = [sends for _, sends, _, _, _ in plan[1:]] + [own_slice]
    *parts, mine, weights = pl.pallas_call(
        functools.partial(query_kernel, out_slices, chunks, blocks, inner, picks),
        out_shape=(in_hbm(flat, width),) * len(out_slices) + (pltpu.VMEM((per_group, full, cand_rows), bf16),),
        in_specs=[SMEM] * 2 + [VMEM] * (3 + len(chunks)),
        out_specs=(ANY,) * len(out_slices) + (VMEM,),
        scratch_shapes=[
            pltpu.VMEM((per_group, full, width), bf16),
            pltpu.VMEM((EXTRA, width), bf16),
            pltpu.SemaphoreType.DMA((per_group + 1, len(out_slices))),
        ],
        compiler_params=params(14),
        cost_estimate=cost(per_group, 1),
        name="query",
    )(pos_arr, id_flat, cands, row_lse, col_lse, *logits)
    parts = [first] + parts

    own_grad, far_grad = pl.pallas_call(
        functools.partial(passage_kernel, chunks, picks),
        out_shape=(
            jax.ShapeDtypeStruct((per_group, rows, width), f32),
            in_hbm(groups, packed, width),
        ),
        in_specs=[SMEM] + [VMEM] * (2 + len(chunks)),
        out_specs=(ANY, ANY),
        scratch_shapes=[
            pltpu.VMEM((per_group, rows, width), f32),
            pltpu.VMEM((slot_count, rows, width), f32),
            pltpu.VMEM((groups, packed, width), bf16),
            pltpu.SemaphoreType.DMA((groups + per_group,)),
        ],
        compiler_params=params(28),
        cost_estimate=cost(per_group, 1),
        name="passage",
    )(slot_flat, row_lse, resident(weights), *wholes)

    sums = []
    for (pairs, _, adds, gates, _), out in zip(plan, parts):
        if adds is not None:
            arrived_sum = jnp.where(one_of(pos, adds[1]), sums[adds[0]].astype(f32), 0.0)
            out = (out.astype(f32) + arrived_sum).astype(bf16)
        if gates:
            out = after(out, *[sums[g] for g in gates])
        sums.append(lax.ppermute(out, "inner", pairs))
    finals = [(devices, value) for (_, _, _, _, devices), value in zip(plan, sums) if devices]

    far_grad = after(far_grad, sums[0])
    returned = lax.all_to_all(far_grad, "dp", split_axis=0, concat_axis=0, tiled=True)
    dest = jnp.where(live_for, sends_for, per_group).reshape(-1)
    query_grad, passage_grad, total = pl.pallas_call(
        functools.partial(finish_kernel, CAP, inner, [devices for devices, _ in finals]),
        out_shape=(
            jax.ShapeDtypeStruct((per_group, rows, width), bf16),
            jax.ShapeDtypeStruct((per_group, rows, width), bf16),
            jax.ShapeDtypeStruct((8, 128), f32),
        ),
        in_specs=[SMEM] * 2 + [VMEM] * 2 + [ANY] * (1 + len(finals)),
        out_specs=(VMEM,) * 3,
        scratch_shapes=[
            pltpu.VMEM((per_group + 1, rows, width), f32),
            pltpu.VMEM((groups, packed, width), bf16),
            pltpu.VMEM((len(finals), flat, width), bf16),
            pltpu.SemaphoreType.DMA((groups,)),
            pltpu.SemaphoreType.DMA((len(finals),)),
        ],
        compiler_params=params(28),
        name="finish",
    )(pos_arr, dest, mine, own_grad, returned, *[value for _, value in finals])
    mean_loss = total[0, 0] / (2.0 * groups * per_group * full)
    return (mean_loss, query_grad, passage_grad)


def solution(mesh):
    in_specs = (P("dp", "inner", None), P("dp", "inner", None), P())
    out_specs = (P(), P("dp", "inner", None), P("dp", "inner", None))
    return jax.shard_map(body, mesh=mesh, in_specs=in_specs, out_specs=out_specs, check_vma=False)
```

```python
import functools
import math

import jax
import jax.numpy as jnp
from jax import lax
from jax.experimental import pallas as pl
from jax.experimental.pallas import tpu as pltpu
from jax.sharding import PartitionSpec as P

CAP = 2
NEG_FILL = -1e30
LOG2E = math.log2(math.e)
LN2 = math.log(2.0)
ANY = pl.BlockSpec(memory_space=pl.ANY)
SMEM = pl.BlockSpec(memory_space=pltpu.SMEM)
VMEM = pl.BlockSpec(memory_space=pltpu.VMEM)
EXTRA = 16
GROUPED = 3
MIB = 1024 * 1024
MARK = 60_000_000_000


def slot_tables(neg_lists, groups, per_group, slot_depth):
    block_count = neg_lists.shape[0]
    block_ids = jnp.arange(block_count, dtype=jnp.int32)
    named = jnp.any(neg_lists[:, :, None] == block_ids[None, None, :], axis=1)
    present = jnp.any(named.reshape(groups, per_group, block_count), axis=1)
    present = present.reshape(groups, groups, per_group).astype(jnp.int32)
    slot_ranks = jnp.cumsum(present, axis=2) - 1
    slot_ids = jnp.arange(slot_depth, dtype=jnp.int32)
    hits = (present[..., None] == 1) & (slot_ranks[..., None] == slot_ids[None, None, None, :])
    local_ids = jnp.arange(per_group, dtype=jnp.int32)
    slot_block = jnp.sum(jnp.where(hits, local_ids[None, None, :, None], 0), axis=2)
    slot_live = jnp.any(hits, axis=2)
    return (slot_ranks, slot_block, slot_live)


def join_log2(a, b):
    return jnp.maximum(a, b) + jnp.log2(1.0 + jnp.exp2(-jnp.abs(a - b)))


def row_tile(rows):
    return math.gcd(rows, 256)


def dot_t(a, b):
    return lax.dot_general(a, b, (((1,), (1,)), ((), ())), preferred_element_type=jnp.float32)


def dot_n(a, b):
    return lax.dot_general(a, b, (((0,), (0,)), ((), ())), preferred_element_type=jnp.float32)


def cand_copy(own_p, far_p, slot_ref, picks, block, k, dst, sem):
    rows = own_p.shape[1]
    src = own_p.at[block] if k == 0 else far_p.at[slot_ref[block * picks + k - 1]]
    return pltpu.make_async_copy(src, dst.at[pl.ds(k * rows, rows)], sem)


def query_copies(block, chunk, pos, own_q, from_left, from_right, dst, sems, arrive):
    first, inner = chunk[0], len(from_left) + 1
    rows = own_q.shape[1]

    def piece(src, at, k):
        return pltpu.make_async_copy(src, dst.at[pl.ds(pl.multiple_of(at * rows, rows), rows)], sems.at[k])

    if arrive:
        for k in range(inner):
            piece(own_q.at[block], k, k).wait()
        return
    piece(own_q.at[block], pos, 0).start()
    for k in range(1, inner):
        @pl.when(pos >= k)
        def _():
            piece(from_left[k - 1].at[block - first], pos - k, k).start()

        @pl.when(pos < k)
        def _():
            piece(from_right[inner - k - 1].at[block - first], pos - k + inner, k).start()


def collect_kernel(picks, slot_ref, own_p, far_p, cands, sems):
    copies = [
        cand_copy(own_p, far_p, slot_ref, picks, b, k, cands.at[b], sems.at[b, k])
        for b in range(cands.shape[0])
        for k in range(picks + 1)
    ]
    for copy in copies:
        copy.start()
    for copy in copies:
        copy.wait()


def forward_kernel(chunk, inner, picks, scale, *refs):
    pos_ref, id_ref, own_q = refs[:3]
    from_left = refs[3:2 + inner]
    from_right = refs[2 + inner:1 + 2 * inner]
    cands, col_in, row_out, col_out, l_out, whole_q, q_sems = refs[1 + 2 * inner:]
    rows = own_q.shape[1]
    full = rows * inner
    tile = row_tile(full)
    pos = pos_ref[0]
    first, count = chunk

    def queries(b, arrive):
        query_copies(first + b, chunk, pos, own_q, from_left, from_right, whole_q.at[b], q_sems.at[b], arrive)

    for b in range(count):
        queries(b, False)
    col_out[...] = col_in[...]
    for b in range(count):
        queries(b, True)
        block_col = None
        for t in range(full // tile):
            logits = dot_t(whole_q[b, t * tile:(t + 1) * tile, :], cands[first + b]) * scale
            l_out[b, t * tile:(t + 1) * tile] = logits
            peak = jnp.max(logits, axis=1, keepdims=True)
            mass = jnp.sum(jnp.exp2(logits - peak), axis=1, keepdims=True)
            row_lse = jnp.broadcast_to(peak + jnp.log2(mass), (tile, 128))
            row_out[b:b + 1, t * tile:(t + 1) * tile] = row_lse.T[0:1, :]
            col_peak = jnp.max(logits, axis=0, keepdims=True)
            col_mass = jnp.sum(jnp.exp2(logits - col_peak), axis=0, keepdims=True)
            col_lse = col_peak + jnp.log2(col_mass)
            block_col = col_lse if block_col is None else join_log2(block_col, col_lse)
        for k in range(picks + 1):
            row = pl.ds(id_ref[(first + b) * (picks + 1) + k], 1)
            col_out[row, :] = join_log2(col_out[row, :], block_col[:, k * rows:(k + 1) * rows])


def scatter_plan(inner):
    if inner == 4:
        return [
            (((0, 1), (3, 2), (2, 0), (1, 3)), {0: 2, 3: 1, 2: 0, 1: 3}, None, (), (0, 3)),
            (((2, 1), (1, 2), (3, 0), (0, 3)), {2: 1, 1: 2, 3: 0, 0: 3}, (0, (1, 2)), (0,), (0, 1, 2, 3)),
            (((0, 1), (1, 0), (2, 3), (3, 2)), {0: 1, 1: 0, 2: 3, 3: 2}, None, (0,), (0, 1, 2, 3)),
        ]
    plan, place = [], {}
    for m in range(inner - 1):
        for t in range(inner - 1 - m):
            place[(t, m)] = len(plan)
            pairs = ((t, t + 1), (inner - 1 - t, inner - 2 - t))
            sends = {t: inner - 1 - m, inner - 1 - t: m}
            adds = (place[(t - 1, m)], tuple(sends)) if t else None
            plan.append((pairs, sends, adds, (), (t + 1, inner - 2 - t) if m == inner - 2 - t else ()))
    return plan


def one_of(pos, devices):
    return functools.reduce(jnp.logical_or, [pos == d for d in devices])


def slice_for(pos, sends):
    at = 0
    for device, target in sends.items():
        at = jnp.where(pos == device, target, at)
    return at


def in_pieces(value, width, lane):
    high = value.astype(jnp.bfloat16).astype(jnp.float32)
    mid = (value - high).astype(jnp.bfloat16).astype(jnp.float32)
    low = value - high - mid
    at = lax.broadcasted_iota(jnp.int32, (EXTRA, width), 1) - lane
    pieces = jnp.where(at == 0, high, jnp.where(at == 1, mid, jnp.where(at == 2, low, 0.0)))
    return pieces.astype(jnp.bfloat16)


def column_lse(b, picks, id_ref, col_lse):
    return jnp.concatenate(
        [col_lse[pl.ds(id_ref[b * (picks + 1) + k], 1), :] for k in range(picks + 1)], axis=1
    ) + 1.0


def block_weights(logits, row, col, first_row, rows, w_ref):
    probs = jnp.exp2(logits - row) + jnp.exp2(logits - col)
    r_id = lax.broadcasted_iota(jnp.int32, (logits.shape[0], rows), 0) + first_row
    c_id = lax.broadcasted_iota(jnp.int32, (logits.shape[0], rows), 1)
    target = jnp.where(r_id == c_id, 1.0, 0.0)
    w_ref[:, 0:rows] = (probs[:, 0:rows] - target).astype(jnp.bfloat16)
    w_ref[:, rows:] = probs[:, rows:].astype(jnp.bfloat16)


def loss_piece(blocks, pos, col_lse, width):
    value = jnp.sum(col_lse[0:blocks, :]) * LN2 - 2.0 * jnp.sum(col_lse[blocks:blocks + 1, 0:1])
    return in_pieces(value, width, 3 * pos)


def early_kernel(sends, chunks, blocks, inner, picks, *refs):
    pos_ref, id_ref, cands, row_lse, col_lse = refs[:5]
    l_refs = refs[5:5 + len(chunks)]
    out, w_buf, row_buf, dq_buf, sems = refs[5 + len(chunks):]
    per_group, full = row_lse.shape
    rows = full // inner
    width = out.shape[1]
    pos = pos_ref[0]
    at = slice_for(pos, sends)
    start = pl.multiple_of(at * rows, rows)
    home = {first + n: (c, n) for c, (first, size) in enumerate(chunks) for n in range(size)}
    dq_buf[per_group * rows:] = loss_piece(blocks, pos, col_lse, width)

    def copy(b):
        part = pl.ds(b * rows, rows if b < per_group else EXTRA)
        return pltpu.make_async_copy(dq_buf.at[part], out.at[part], sems.at[b])

    copy(per_group).start()
    for b in range(per_group):
        c, n = home[b]
        row_buf[...] = jnp.broadcast_to(row_lse[b:b + 1, :] + 1.0, (128, full)).T
        block_weights(
            l_refs[c][n, pl.ds(start, rows), :], row_buf[pl.ds(start, rows), 0:1],
            column_lse(b, picks, id_ref, col_lse), (at - pos) * rows, rows, w_buf.at[b],
        )
        grad = jnp.dot(w_buf[b], cands[b], preferred_element_type=jnp.float32)
        dq_buf[b * rows:(b + 1) * rows] = grad.astype(jnp.bfloat16)
        copy(b).start()
    for b in range(per_group + 1):
        copy(b).wait()


def query_kernel(out_slices, chunks, blocks, inner, picks, *refs):
    pos_ref, id_ref, cands, row_lse, col_lse = refs[:5]
    l_refs = refs[5:5 + len(chunks)]
    refs = refs[5 + len(chunks):]
    outs = refs[:len(out_slices)]
    w_buf, dq_buf, piece_buf, dq_sems = refs[len(out_slices):]
    per_group, full, width = dq_buf.shape
    rows = full // inner
    tile = row_tile(full)
    pos = pos_ref[0]
    home = {at + n: (c, n) for c, (at, size) in enumerate(chunks) for n in range(size)}

    def outgoing(b, act):
        for n, (out, sends) in enumerate(zip(outs, out_slices)):
            @pl.when(one_of(pos, sends))
            def _():
                if b < per_group:
                    at = pl.multiple_of(slice_for(pos, sends) * rows, rows)
                    src, dst = dq_buf.at[b, pl.ds(at, rows)], out.at[pl.ds(b * rows, rows)]
                else:
                    src, dst = piece_buf, out.at[pl.ds(per_group * rows, EXTRA)]
                copy = pltpu.make_async_copy(src, dst, dq_sems.at[b, n])
                copy.wait() if act == "wait" else copy.start()

    piece_buf[...] = loss_piece(blocks, pos, col_lse, width)
    outgoing(per_group, "start")
    for b in range(per_group):
        c, n = home[b]
        col = column_lse(b, picks, id_ref, col_lse)
        row = jnp.broadcast_to(row_lse[b:b + 1, :] + 1.0, (128, full)).T
        for t in range(full // tile):
            part = slice(t * tile, (t + 1) * tile)
            block_weights(
                l_refs[c][n, part, :], row[part, 0:1], col, t * tile - pos * rows, rows, w_buf.at[b, part]
            )
            grad = jnp.dot(w_buf[b, part, :], cands[b], preferred_element_type=jnp.float32)
            dq_buf[b, part] = grad.astype(jnp.bfloat16)
        outgoing(b, "start")
    for b in range(per_group + 1):
        outgoing(b, "wait")


def passage_kernel(chunks, picks, *refs):
    slot_ref, row_lse, weights = refs[:3]
    q_refs = refs[3:3 + len(chunks)]
    own_out, far_out, far_acc, far_buf, far_sems = refs[3 + len(chunks):]
    per_group, rows, width = own_out.shape
    groups, packed = far_buf.shape[:2]
    depth = packed // rows
    home = {at + n: (c, n) for c, (at, size) in enumerate(chunks) for n in range(size)}

    far_acc[...] = jnp.zeros_like(far_acc)
    for b in range(per_group):
        c, n = home[b]
        step = math.gcd(picks + 1, GROUPED)
        for k in range(0, picks + 1, step):
            parts = dot_n(weights[b, :, k * rows:(k + step) * rows], q_refs[c][n])
            for j in range(step):
                part = parts[j * rows:(j + 1) * rows]
                if k + j == 0:
                    own_out[b] = part
                else:
                    slot = slot_ref[b * picks + k + j - 1]
                    far_acc[slot] = far_acc[slot] + part
    row_pieces = in_pieces(jnp.sum(row_lse[0:per_group, :]) * LN2, width, 0)
    for g in range(groups):
        for c in range(depth):
            far_buf[g, c * rows:(c + 1) * rows] = far_acc[g * depth + c].astype(jnp.bfloat16)
        far_buf[g, depth * rows:] = row_pieces
        pltpu.make_async_copy(far_buf.at[g], far_out.at[g], far_sems.at[g]).start()
    for g in range(groups):
        pltpu.make_async_copy(far_buf.at[g], far_out.at[g], far_sems.at[g]).wait()


def finish_kernel(depth, inner, finals, pos_ref, dest_ref, mine_ref, own_ref, far_ref, *refs):
    moved = refs[:len(finals)]
    q_out, p_out, loss_ref, acc, got, q_got, q_buf, p_buf, sems, q_sems, out_sems = refs[len(finals):]
    groups = far_ref.shape[0]
    per_group, rows, _ = p_out.shape
    pos = pos_ref[0]

    def far_copy(g):
        return pltpu.make_async_copy(far_ref.at[g], got.at[g], sems.at[g])

    def moved_copy(n, b):
        part = pl.ds(b * rows, rows if b < per_group else EXTRA)
        return pltpu.make_async_copy(moved[n].at[part], q_got.at[n, part], q_sems.at[n, b])

    def q_copy(b):
        return pltpu.make_async_copy(q_buf.at[b], q_out.at[b], out_sems.at[0, b])

    def p_copy(b):
        return pltpu.make_async_copy(p_buf.at[b], p_out.at[b], out_sems.at[1, b])

    for b in range(per_group + 1):
        for n, devices in enumerate(finals):
            @pl.when(one_of(pos, devices))
            def _():
                moved_copy(n, b).start()
    for g in range(groups):
        far_copy(g).start()
    ends = {}
    for d in range(inner):
        ends.setdefault(tuple(n for n, devices in enumerate(finals) if d in devices), []).append(d)
    lane = lax.broadcasted_iota(jnp.int32, (8, 128), 1)
    acc[0:per_group] = own_ref[...]
    for which, devices in ends.items():
        @pl.when(one_of(pos, devices))
        def _():
            for b in range(per_group):
                part = slice(b * rows, (b + 1) * rows)
                value = mine_ref[part, :].astype(jnp.float32)
                for n in which:
                    moved_copy(n, b).wait()
                    value = value + q_got[n, part, :].astype(jnp.float32)
                q_buf[b] = value.astype(jnp.bfloat16)
                q_copy(b).start()
            piece = mine_ref[per_group * rows:, 0:128].astype(jnp.float32)
            for n in which:
                moved_copy(n, per_group).wait()
                piece = piece + q_got[n, per_group * rows:, 0:128].astype(jnp.float32)
            loss_ref[...] = jnp.where(lane < 3 * inner, piece[0:8], 0.0)
    pieces = loss_ref[...]
    for g in range(groups):
        far_copy(g).wait()
        for c in range(depth):
            dest = dest_ref[g * depth + c]
            acc[dest] = acc[dest] + got[g, c * rows:(c + 1) * rows].astype(jnp.float32)
        pieces = pieces + got[g, depth * rows:, 0:128].astype(jnp.float32)[0:8]
    for b in range(per_group):
        p_buf[b] = acc[b].astype(jnp.bfloat16)
        p_copy(b).start()
    total = jnp.sum(pieces, axis=1, keepdims=True) * (0.5 / (groups * per_group * rows * inner))
    loss_ref[...] = total + jnp.zeros((8, 128), jnp.float32)
    for b in range(per_group):
        q_copy(b).wait()
        p_copy(b).wait()


def mark_kernel(a_ref, b_ref, out_ref):
    del a_ref, b_ref
    out_ref[...] = jnp.zeros_like(out_ref)


def after(value, *events):
    return lax.optimization_barrier((value, *events))[0]


def doublings(size):
    return [1 << n for n in range(size.bit_length() - 1)]


def butterfly(value, axis, size, join):
    for step in doublings(size):
        other = lax.ppermute(value, axis, [(i, i ^ step) for i in range(size)])
        value = join(value, other)
    return value


def body(queries, passages, neg_lists):
    per_group, rows, width = queries.shape
    picks = neg_lists.shape[1]
    blocks = neg_lists.shape[0]
    groups = lax.axis_size("dp")
    inner = lax.axis_size("inner")
    full = rows * inner
    cand_rows = (picks + 1) * rows
    slot_count = groups * CAP
    scale = 1.0 / math.sqrt(width)
    my_group = lax.axis_index("dp")
    pos = lax.axis_index("inner")
    f32, bf16 = jnp.float32, jnp.bfloat16

    def params(mib):
        return pltpu.CompilerParams(vmem_limit_bytes=mib * MIB)

    def in_hbm(*shape):
        return pltpu.HBM(shape, bf16)

    def resident(value):
        return pltpu.with_memory_space_constraint(value, pltpu.VMEM)

    block_flops = 2 * full * cand_rows * width
    block_bytes = 2 * (full + cand_rows) * width

    def cost(blocks, products):
        return pl.CostEstimate(
            flops=blocks * products * block_flops, bytes_accessed=blocks * products * block_bytes, transcendentals=0
        )

    half = per_group // 2
    chunks = [(0, half), (half, per_group - half)]
    lefts = [[] for _ in chunks]
    rights = [[] for _ in chunks]
    moving = [[queries[at:at + size]] * 2 for at, size in chunks]
    for s in range(1, inner):
        for c in range(len(chunks)):
            moving[c] = [
                lax.ppermute(moving[c][0], "inner", [(i, i + 1) for i in range(s - 1, inner - 1)]),
                lax.ppermute(moving[c][1], "inner", [(i, i - 1) for i in range(inner - s, 0, -1)]),
            ]
            lefts[c].append(moving[c][0])
            rights[c].append(moving[c][1])
            if s == 1:
                mark = pl.pallas_call(
                    mark_kernel,
                    out_shape=jax.ShapeDtypeStruct((8, 128), f32),
                    in_specs=[ANY, ANY],
                    out_specs=VMEM,
                    compiler_params=params(1),
                    cost_estimate=pl.CostEstimate(flops=MARK, bytes_accessed=0, transcendentals=0),
                    name="mark",
                )(*moving[c])
                moving[c] = [after(value, mark) for value in moving[c]]

    slot_ranks, slot_block, slot_live = slot_tables(neg_lists, groups, per_group, CAP)
    listed = lax.dynamic_slice_in_dim(neg_lists, my_group * per_group, per_group, 0)
    my_ranks = lax.dynamic_index_in_dim(slot_ranks, my_group, 0, keepdims=False)
    slot_of = (listed // per_group) * CAP + my_ranks[listed // per_group, listed % per_group]
    slot_flat = slot_of.reshape(-1)
    own_ids = my_group * per_group + jnp.arange(per_group, dtype=jnp.int32)
    id_flat = jnp.concatenate([own_ids[:, None], listed], axis=1).reshape(-1)
    pos_arr = pos.reshape(1)
    sends_for = lax.dynamic_index_in_dim(slot_block, my_group, 1, keepdims=False)
    live_for = lax.dynamic_index_in_dim(slot_live, my_group, 1, keepdims=False)
    outgoing = passages[sends_for]
    arrived = lax.all_to_all(outgoing, "dp", split_axis=0, concat_axis=0, tiled=True)
    arrived = arrived.reshape(slot_count, rows, width)

    own_sum = jnp.sum(queries.astype(f32) * passages.astype(f32)) * scale
    col = jnp.concatenate([jnp.full((blocks, rows), NEG_FILL, f32), jnp.broadcast_to(own_sum, (8, rows))])
    cands = pl.pallas_call(
        functools.partial(collect_kernel, picks),
        out_shape=pltpu.VMEM((per_group, cand_rows, width), bf16),
        in_specs=[SMEM, ANY, ANY],
        out_specs=VMEM,
        scratch_shapes=[pltpu.SemaphoreType.DMA((per_group, picks + 1))],
        compiler_params=params(2),
        name="collect",
    )(slot_flat, passages, arrived)
    cands = resident(cands)
    row_parts, logits, wholes = [], [], []
    for c, chunk in enumerate(chunks):
        row_part, col, logit, whole = pl.pallas_call(
            functools.partial(forward_kernel, chunk, inner, picks, scale * LOG2E),
            out_shape=(
                jax.ShapeDtypeStruct((chunk[1], full), f32),
                jax.ShapeDtypeStruct(col.shape, f32),
                pltpu.VMEM((chunk[1], full, cand_rows), f32),
                pltpu.VMEM((chunk[1], full, width), bf16),
            ),
            in_specs=[SMEM] * 2 + [ANY] * (2 * inner - 1) + [VMEM] * 2,
            out_specs=(VMEM,) * 4,
            scratch_shapes=[pltpu.SemaphoreType.DMA((chunk[1], inner))],
            compiler_params=params(12),
            cost_estimate=cost(chunk[1], 1),
            name=f"forward_{c}",
        )(pos_arr, id_flat, queries, *lefts[c], *rights[c], cands, col)
        row_parts.append(row_part)
        logits.append(resident(logit))
        wholes.append(resident(whole))
    row = jnp.concatenate(row_parts, axis=0)
    is_lse = jnp.arange(blocks + 8)[:, None] < blocks
    col_lse = butterfly(col, "dp", groups, lambda a, b: jnp.where(is_lse, join_log2(a, b), a + b))
    row_lse = butterfly(row, "inner", inner, join_log2)

    packed = CAP * rows + EXTRA
    flat = per_group * rows + EXTRA
    plan = scatter_plan(inner)
    first = pl.pallas_call(
        functools.partial(early_kernel, plan[0][1], chunks, blocks, inner, picks),
        out_shape=in_hbm(flat, width),
        in_specs=[SMEM] * 2 + [VMEM] * (3 + len(chunks)),
        out_specs=ANY,
        scratch_shapes=[
            pltpu.VMEM((per_group, rows, cand_rows), bf16),
            pltpu.VMEM((full, 128), f32),
            pltpu.VMEM((flat, width), bf16),
            pltpu.SemaphoreType.DMA((per_group + 1,)),
        ],
        compiler_params=params(12),
        cost_estimate=cost(1, 1),
        name="early",
    )(pos_arr, id_flat, cands, row_lse, col_lse, *logits)
    own_slice = {d: d for d in range(inner)}
    out_slices = [sends for _, sends, _, _, _ in plan[1:]] + [own_slice]
    *parts, mine, weights = pl.pallas_call(
        functools.partial(query_kernel, out_slices, chunks, blocks, inner, picks),
        out_shape=(in_hbm(flat, width),) * (len(out_slices) - 1)
        + (pltpu.VMEM((flat, width), bf16), pltpu.VMEM((per_group, full, cand_rows), bf16)),
        in_specs=[SMEM] * 2 + [VMEM] * (3 + len(chunks)),
        out_specs=(ANY,) * (len(out_slices) - 1) + (VMEM, VMEM),
        scratch_shapes=[
            pltpu.VMEM((per_group, full, width), bf16),
            pltpu.VMEM((EXTRA, width), bf16),
            pltpu.SemaphoreType.DMA((per_group + 1, len(out_slices))),
        ],
        compiler_params=params(14),
        cost_estimate=cost(per_group, 1),
        name="query",
    )(pos_arr, id_flat, cands, row_lse, col_lse, *logits)
    parts = [first] + parts

    own_grad, far_grad = pl.pallas_call(
        functools.partial(passage_kernel, chunks, picks),
        out_shape=(
            pltpu.VMEM((per_group, rows, width), f32),
            in_hbm(groups, packed, width),
        ),
        in_specs=[SMEM] + [VMEM] * (2 + len(chunks)),
        out_specs=(VMEM, ANY),
        scratch_shapes=[
            pltpu.VMEM((slot_count, rows, width), f32),
            pltpu.VMEM((groups, packed, width), bf16),
            pltpu.SemaphoreType.DMA((groups,)),
        ],
        compiler_params=params(28),
        cost_estimate=cost(per_group, 1),
        name="passage",
    )(slot_flat, row_lse, resident(weights), *wholes)

    sums = []
    for (pairs, _, adds, gates, _), out in zip(plan, parts):
        if adds is not None:
            arrived_sum = jnp.where(one_of(pos, adds[1]), sums[adds[0]].astype(f32), 0.0)
            out = (out.astype(f32) + arrived_sum).astype(bf16)
        if gates:
            out = after(out, *[sums[g] for g in gates])
        sums.append(lax.ppermute(out, "inner", pairs))
    finals = [(devices, value) for (_, _, _, _, devices), value in zip(plan, sums) if devices]

    far_grad = after(far_grad, sums[0])
    returned = lax.all_to_all(far_grad, "dp", split_axis=0, concat_axis=0, tiled=True)
    dest = jnp.where(live_for, sends_for, per_group).reshape(-1)
    query_grad, passage_grad, total = pl.pallas_call(
        functools.partial(finish_kernel, CAP, inner, [devices for devices, _ in finals]),
        out_shape=(
            jax.ShapeDtypeStruct((per_group, rows, width), bf16),
            jax.ShapeDtypeStruct((per_group, rows, width), bf16),
            jax.ShapeDtypeStruct((8, 128), f32),
        ),
        in_specs=[SMEM] * 2 + [VMEM] * 2 + [ANY] * (1 + len(finals)),
        out_specs=(ANY, ANY, VMEM),
        scratch_shapes=[
            pltpu.VMEM((per_group + 1, rows, width), f32),
            pltpu.VMEM((groups, packed, width), bf16),
            pltpu.VMEM((len(finals), flat, width), bf16),
            pltpu.VMEM((per_group, rows, width), bf16),
            pltpu.VMEM((per_group, rows, width), bf16),
            pltpu.SemaphoreType.DMA((groups,)),
            pltpu.SemaphoreType.DMA((len(finals), per_group + 1)),
            pltpu.SemaphoreType.DMA((2, per_group)),
        ],
        compiler_params=params(28),
        name="finish",
    )(pos_arr, dest, resident(mine), resident(own_grad), returned, *[value for _, value in finals])
    return (total[0, 0], query_grad, passage_grad)


def solution(mesh):
    in_specs = (P("dp", "inner", None), P("dp", "inner", None), P())
    out_specs = (P(), P("dp", "inner", None), P("dp", "inner", None))
    return jax.shard_map(body, mesh=mesh, in_specs=in_specs, out_specs=out_specs, check_vma=False)
```
